512 devices in a mesh: pool: 64 (over z, x), con: 8 (over y, core).
Axes of the slice: x: 4, y: 4, z: 16, core: 2. Of those that a mesh axis runs over, the one named last changes fastest.
Arguments:
- pool_feat: bfloat16 [32768, 64], P('pool'), may hold values from -5 to 5
- contract_feat: bfloat16 [32768, 64], P('con'), may hold values from -5 to 5
- supply: float32 [32768], P('pool'), may hold values from 0.3 to 4
- caps: int32 [32768], P('con'), may hold values from 1 to 16
- eligible: int32 [256, 256], P('pool', 'con'), may hold values from 0 to 1, as said below
- grad_log_pool: float32 [32768], P('pool'), may hold values from -48 to 48
- grad_log_contract: float32 [32768], P('con'), may hold values from -48 to 48
Outputs:
- pool_grad: float32 [32768, 64], P('pool')
- contract_grad: float32 [32768, 64], P('con')
The draws below stay inside these ranges and needn't reach their ends.
Inputs may be any that keep to these rules, and one draw needn't show every extreme that they name: `eligible`: values are 0 or 1; every row of tiles and every column of tiles holds at least one 1.
All inputs are finite; a program needn't handle non-finite values.
Results may differ from the reference program's by a relative error of at most 0.0026.
Values sent between devices are 32-bit elements; how exact they have to be, the bound alone decides.
No kernel may reach another device: no remote copies, remote signals or barrier semaphores. Data moves between devices by JAX's collectives and lax.ppermute only.
A program may use at most 64 MiB of HBM per device.

```python
import math
import jax
import jax.numpy as jnp
from jax import lax

F = 64
TILE = 128
ITERS = 2
COLS_DEV = 4096
POOLS = 32768
CONTRACTS = 32768


def draw_eligible(key, part):
    row_tiles = POOLS // TILE
    col_tiles = CONTRACTS // TILE
    random_part = (jax.random.randint(key, (row_tiles, col_tiles), 0, 5) < 3).astype(jnp.int32)
    row_index = jnp.arange(row_tiles, dtype=jnp.int32)[:, None]
    col_index = jnp.arange(col_tiles, dtype=jnp.int32)[None, :]
    forced = jnp.logical_or(col_index % row_tiles == row_index, row_index % col_tiles == col_index)
    return jnp.maximum(random_part, forced.astype(jnp.int32))


def touch_ends(drawn, key, low, largest):
    longest = drawn.shape.index(max(drawn.shape))
    spots = []
    for shift in (0, 1):
        where = [jax.random.randint(jax.random.fold_in(key, axis), (), 0, length) for axis, length in enumerate(drawn.shape)]
        where[longest] = (where[longest] + shift) % drawn.shape[longest]
        spots.append(tuple(where))
    return drawn.at[spots[0]].set(low).at[spots[1]].set(largest)


def levels(rng, dims, split, least, largest):
    loudness, own = 1.0, jax.random.fold_in(rng, 6)
    for axis_at, blocks in split:
        draws = jnp.exp(jax.random.uniform(jax.random.fold_in(own, axis_at), (blocks,), jnp.float32, least / len(split), largest / len(split)))
        loudness = loudness * jnp.repeat(draws, dims[axis_at] // blocks).reshape([-1 if axis == axis_at else 1 for axis in range(len(dims))])
    return loudness


def bell_draw(rng, dims, spread, limit, shards=(), kind=jnp.bfloat16):
    level = levels(rng, dims, shards, -0.22, 0.18) if shards else 1.0
    drawn = jax.random.normal(rng, dims, jnp.float32) * spread * level
    return jnp.minimum(jnp.maximum(drawn, -limit), limit).astype(kind)


def setup_inputs(seed: int = 0) -> dict:
    arg_keys = jax.random.split(jax.random.key(seed), 8)
    pool_feat = bell_draw(arg_keys[0], (POOLS, F), 1.0, 5.0, ((0, 64),))
    contract_feat = bell_draw(arg_keys[1], (CONTRACTS, F), 1.0, 5.0, ((0, 8),))
    supply = jnp.clip(jnp.exp(math.log(4.0) - 2.5902671 * jax.random.uniform(arg_keys[2], (POOLS,), jnp.float32) ** levels(arg_keys[2], (POOLS,), ((0, 64),), -0.2, 0.2)), 0.3, 4.0)
    caps = touch_ends(jax.random.randint(arg_keys[3], (CONTRACTS,), 1, 17), jax.random.fold_in(arg_keys[3], 1), 1, 16).astype(jnp.int32)
    eligible = draw_eligible(jax.random.fold_in(arg_keys[7], 71), 0)
    grad_log_pool = bell_draw(arg_keys[5], (POOLS,), 8.0, 48.0, ((0, 64),), jnp.float32)
    grad_log_contract = bell_draw(arg_keys[6], (CONTRACTS,), 8.0, 48.0, ((0, 8),), jnp.float32)
    return dict(pool_feat=pool_feat, contract_feat=contract_feat, supply=supply, caps=caps, eligible=eligible, grad_log_pool=grad_log_pool, grad_log_contract=grad_log_contract)


HIGHEST_PRECISION = lax.Precision.HIGHEST


def kernel_tile(pool_feat, feat_block, mask_block):
    scores = jnp.dot(pool_feat, feat_block.T, preferred_element_type=jnp.float32) * 0.125
    values = jnp.exp(scores)
    row_count, col_count = values.shape
    shaped = values.reshape(row_count // TILE, TILE, col_count // TILE, TILE) * mask_block.astype(jnp.float32)[:, None, :, None]
    return shaped.reshape(row_count, col_count)


def reference(pool_feat, contract_feat, supply, caps, eligible, grad_log_pool, grad_log_contract):
    block_width = min(1024, COLS_DEV)
    blocks = CONTRACTS // block_width
    feat_blocks = contract_feat.reshape(blocks, block_width, F)
    mask_blocks = eligible.reshape(POOLS // TILE, blocks, block_width // TILE).transpose(1, 0, 2)
    demand = caps.astype(jnp.float32)

    def column_sums(weights):
        def per_block(entries):
            return jnp.dot(weights, kernel_tile(pool_feat, entries[0], entries[1]), precision=HIGHEST_PRECISION)
        return lax.map(per_block, (feat_blocks, mask_blocks)).reshape(CONTRACTS)

    def row_sums(weights):
        weight_blocks = weights.reshape(blocks, block_width)

        def per_block(summed, entries):
            kernel = kernel_tile(pool_feat, entries[0], entries[1])
            return summed + jnp.dot(kernel, entries[2], precision=HIGHEST_PRECISION), None
        summed, _ = lax.scan(per_block, jnp.zeros((POOLS,), jnp.float32), (feat_blocks, mask_blocks, weight_blocks))
        return summed

    pool_scale = jnp.ones((POOLS,), jnp.float32)
    earlier = []
    contract_scales = []
    row_results = []
    for iteration in range(ITERS):
        earlier.append(pool_scale)
        contract_scale = demand / column_sums(pool_scale)
        row_total = row_sums(contract_scale)
        pool_scale = supply / row_total
        contract_scales.append(contract_scale)
        row_results.append(row_total)

    row_adj = -grad_log_pool / row_results[-1]
    left_parts = []
    right_parts = []
    for iteration in reversed(range(ITERS)):
        summed = column_sums(row_adj)
        contract_scale = contract_scales[iteration]
        if iteration == ITERS - 1:
            col_adj = -(grad_log_contract / contract_scale + summed) * contract_scale * contract_scale / demand
        else:
            col_adj = -summed * contract_scale * contract_scale / demand
        left_parts += [row_adj, earlier[iteration]]
        right_parts += [contract_scale, col_adj]
        if iteration > 0:
            pool_adj = row_sums(col_adj)
            row_adj = -pool_adj * earlier[iteration] / row_results[iteration - 1]

    left_mat = jnp.stack(left_parts, axis=1)
    right_blocks = jnp.stack(right_parts, axis=1).reshape(blocks, block_width, 2 * ITERS)

    def final_block(carried, entries):
        kernel = kernel_tile(pool_feat, entries[0], entries[1])
        weights = jnp.dot(left_mat, entries[2].T, precision=HIGHEST_PRECISION)
        product = (kernel * weights).astype(jnp.bfloat16)
        carried = carried + jnp.dot(product, entries[0], preferred_element_type=jnp.float32) * 0.125
        column_part = lax.dot_general(product, pool_feat, (((0,), (0,)), ((), ())), preferred_element_type=jnp.float32) * 0.125
        return carried, column_part

    pool_grad, column_blocks = lax.scan(final_block, jnp.zeros((POOLS, F), jnp.float32), (feat_blocks, mask_blocks, right_blocks))
    return pool_grad, column_blocks.reshape(CONTRACTS, F)
```

```python
import jax
import jax.numpy as jnp
from jax import lax
from jax.experimental import pallas as pl
from jax.experimental.pallas import tpu as pltpu
from jax.sharding import PartitionSpec as P

NX = 4
NZ = 16
NCON = 8
NXC = NX * NCON
LANES = 128
F = 64
ROWS_IN = 512
ROWS = NX * ROWS_IN
COLS = 1024
RG = ROWS // LANES
CG = COLS // LANES
TILES_IN = ROWS_IN // LANES
MASK_AT = F + 2
PACK = 80
WIDE = 512
F32 = jnp.float32
BF16 = jnp.bfloat16

ALONG_Z = [[z * NX + x for z in range(NZ)] for x in range(NX)]
ALONG_X = [[z * NX + x for x in range(NX)] for z in range(NZ)]
SAME_Z = [[z * NXC + k for k in range(NXC)] for z in range(NZ)]


def over_z(parts):
    return lax.all_to_all(parts, "pool", 0, 0, tiled=True, axis_index_groups=ALONG_Z)


def over_x(parts):
    return lax.all_to_all(parts, "pool", 0, 0, tiled=True, axis_index_groups=ALONG_X)


def over_con(parts):
    return lax.all_to_all(parts, "con", 0, 0, tiled=True)


def over_rows(parts):
    return lax.all_to_all(
        parts, ("pool", "con"), 0, 0, tiled=True, axis_index_groups=SAME_Z
    )


def call(body, outs, args, scratch=(), smem=(), flops=0, trans=0):
    vmem = pl.BlockSpec(memory_space=pltpu.VMEM)
    nbytes = sum(a.size * a.dtype.itemsize for a in args) + sum(
        o.size * o.dtype.itemsize for o in outs
    )
    return pl.pallas_call(
        body,
        out_shape=outs,
        in_specs=[
            pl.BlockSpec(memory_space=pltpu.SMEM) if i in smem else vmem
            for i in range(len(args))
        ],
        out_specs=[vmem] * len(outs),
        scratch_shapes=list(scratch),
        compiler_params=pltpu.CompilerParams(vmem_limit_bytes=16 * 1024 * 1024),
        cost_estimate=pl.CostEstimate(
            flops=flops, bytes_accessed=nbytes, transcendentals=trans
        ),
    )(*args)


def shape(*dims, dtype=F32):
    return jax.ShapeDtypeStruct(dims, dtype)


def pack_body(feat_t, supply, grad, eligible, out):
    rows = feat_t[...].astype(F32)
    for x in range(NX):
        out[x, :F, :] = rows
        out[x, F : F + 1, :] = supply[...]
        out[x, F + 1 : F + 2, :] = grad[...]
        for k in range(CG):
            for t in range(TILES_IN):
                out[x, MASK_AT + k : MASK_AT + k + 1, t * LANES : (t + 1) * LANES] = (
                    jnp.full((1, LANES), eligible[t, x * CG + k].astype(F32), F32)
                )
        out[x, MASK_AT + CG :, :] = jnp.zeros((PACK - MASK_AT - CG, ROWS_IN), F32)


def put_columns(row, out, copies):
    for k in range(CG):
        piece = row[:, k * LANES : (k + 1) * LANES]
        for w in range(copies):
            out[w, k : k + 1, :] = piece


def kernel_body(packed, cft, kern, kern16, supply, grad, sums, acc):
    width = 256
    acc[...] = jnp.zeros_like(acc)
    for x in range(NX):
        for t in range(TILES_IN):
            at = slice(t * LANES, (t + 1) * LANES)
            g = x * TILES_IN + t
            supply[g : g + 1, :] = packed[x, F : F + 1, at]
            grad[g : g + 1, :] = packed[x, F + 1 : F + 2, at]

    def per_shard(x, _):
        for h in range(2):
            feat = packed[x, :F, h * 256 : h * 256 + 256].T.astype(BF16)
            base = pl.multiple_of(x * ROWS_IN + h * 256, 256)
            for n in range(COLS // width):
                scores = jnp.dot(
                    feat,
                    cft[:, n * width : (n + 1) * width],
                    preferred_element_type=F32,
                )
                values = jnp.exp(scores * 0.125)
                for t in range(2):
                    for j in range(2):
                        k = n * 2 + j
                        tile = h * 2 + t
                        block = (
                            values[t * 128 : t * 128 + 128, j * 128 : j * 128 + 128]
                            * packed[
                                x,
                                MASK_AT + k : MASK_AT + k + 1,
                                tile * 128 : tile * 128 + 128,
                            ]
                        )
                        rows = pl.ds(base + t * 128, 128)
                        kern[rows, k * 128 : k * 128 + 128] = block
                        kern16[rows, k * 128 : k * 128 + 128] = block.astype(BF16)
                        acc[:, k * 128 : k * 128 + 128] += jnp.sum(
                            block.reshape(16, 8, 128), axis=0
                        )
        return 0

    lax.fori_loop(0, NX, per_shard, 0)
    put_columns(jnp.sum(acc[...], axis=0, keepdims=True), sums, NZ)


def row_sums(kern, vec, out, copies):
    def group(g, _):
        rows = pl.ds(pl.multiple_of(g * LANES, LANES), LANES)
        total = kern[rows, 0:LANES] * vec[0:1, :]
        for k in range(1, CG):
            total += kern[rows, k * LANES : (k + 1) * LANES] * vec[k : k + 1, :]
        line = jnp.sum(total.T, axis=0, keepdims=True)
        for w in range(copies):
            out[w, pl.ds(g, 1), :] = line
        return 0

    lax.fori_loop(0, RG, group, 0, unroll=2)


def as_column(vec, g):
    return jnp.broadcast_to(vec[pl.ds(g, 1), :], (LANES, LANES)).T


def column_sums(kern, vec, out, copies, acc):
    acc[...] = jnp.zeros_like(acc)

    def group(g, _):
        rows = pl.ds(pl.multiple_of(g * LANES, LANES), LANES)
        weight = as_column(vec, g)
        for k in range(CG):
            block = kern[rows, k * LANES : (k + 1) * LANES] * weight
            acc[:, k * LANES : (k + 1) * LANES] += jnp.sum(
                block.reshape(16, 8, LANES), axis=0
            )
        return 0

    lax.fori_loop(0, RG, group, 0, unroll=2)
    put_columns(jnp.sum(acc[...], axis=0, keepdims=True), out, copies)


def forward_columns_body(gathered, demand, kern, scale, out):
    scale[...] = demand[...] / jnp.sum(gathered[...], axis=0)
    row_sums(kern, scale, out, NXC)


def adjoint_columns_body(gathered, demand, scale, grad, kern, adj, out):
    s = scale[...]
    summed = jnp.sum(gathered[...], axis=0)
    adj[...] = -(grad[...] / s + summed) * s * s / demand[...]
    row_sums(kern, adj, out, NXC)


def forward_rows_body(gathered, supply, kern, total, scale, out, acc):
    total[...] = jnp.sum(gathered[...], axis=0)
    scale[...] = supply[...] / total[...]
    column_sums(kern, scale, out, NZ, acc)


def first_rows_body(gathered, supply, kern, ones, total, scale, out, acc):
    out[:, :, :WIDE] = ones[...]
    forward_rows_body(gathered, supply, kern, total, scale, out.at[:, :, WIDE:], acc)


def first_columns_body(gathered, demand, kern, scale, owned, out):
    owned[...] = jnp.sum(gathered[:, :, :WIDE], axis=0)
    forward_columns_body(gathered.at[:, :, WIDE:], demand, kern, scale, out)


def last_rows_body(gathered, grad, kern, adj, out, acc):
    adj[...] = -grad[...] / jnp.sum(gathered[...], axis=0)
    column_sums(kern, adj, out, NZ, acc)


def split(value):
    high = value.astype(BF16)
    return high, (value - high.astype(F32)).astype(BF16)


def feature_sums(packed, vec, kern16):
    lines = [
        packed[g // TILES_IN, :F, g % TILES_IN * LANES : (g % TILES_IN + 1) * LANES]
        * vec[g : g + 1, :]
        for g in range(RG)
    ]
    high, low = split(jnp.concatenate(lines, axis=1))
    both = jnp.dot(
        jnp.concatenate([high, low], axis=0), kern16[...], preferred_element_type=F32
    )
    return both[:F] + both[F:]


def put_features(value, out):
    for z in range(NZ):
        f, half = z // 2 * 8, z % 2 * WIDE
        out[z] = value[f : f + 8, half : half + WIDE]


def ones_features_body(packed, kern16, out):
    feat = jnp.concatenate([packed[x, :F, :] for x in range(NX)], axis=1).astype(BF16)
    put_features(jnp.dot(feat, kern16[...], preferred_element_type=F32), out)


def features_body(packed, vec, kern16, out):
    out[...] = feature_sums(packed, vec, kern16)


def as_row(vec):
    return jnp.concatenate([vec[k : k + 1, :] for k in range(CG)], axis=1)


def inner_rows_body(
    gathered, scale, total, kern, kern16, packed, v1, v2, c2, with_adj2, with_u1, adj, out, acc
):
    adj[...] = -jnp.sum(gathered[...], axis=0) * scale[...] / total[...]
    put_features(
        as_row(v2) * with_adj2[...]
        + as_row(c2) * with_u1[...]
        + as_row(v1) * feature_sums(packed, adj, kern16),
        out.at[:, :, :WIDE],
    )
    column_sums(kern, adj, out.at[:, :, WIDE:], NZ, acc)


def owner_body(gathered, ones, v1, demand, c1, out):
    v = v1[...]
    c1[...] = -jnp.sum(gathered[:, :, WIDE:], axis=0) * v * v / demand[...]
    scale = as_row(c1)
    odd = lax.rem(lax.div(lax.axis_index("pool"), NX), 2) == 1
    mine = jnp.where(odd, scale[:, WIDE:], scale[:, :WIDE])
    value = (jnp.sum(gathered[:, :, :WIDE], axis=0) + mine * ones[...]) * 0.125
    for w in range(NZ):
        out[w] = value


def pool_part_body(c1, v1, v2, c2, adj2, u1, adj1, kern, cft, out, prod):
    def shard(x, _):
        for t in range(TILES_IN):
            g = x * TILES_IN + t
            rows = pl.ds(pl.multiple_of(g * LANES, LANES), LANES)
            a2, uu, a1 = as_column(adj2, g), as_column(u1, g), as_column(adj1, g)
            for k in range(CG):
                at = slice(k * LANES, (k + 1) * LANES)
                one = slice(k, k + 1)
                w = a2 * v2[one, :] + uu * c2[one, :] + a1 * v1[one, :] + c1[one, :]
                prod[t * LANES : (t + 1) * LANES, at] = (kern[rows, at] * w).astype(BF16)
        part = lax.dot_general(
            cft[...], prod[...], (((1,), (1,)), ((), ())), preferred_element_type=F32
        )
        for c in range(NCON):
            out[x * NCON + c] = part[c * 8 : c * 8 + 8, :] * 0.125
        return 0

    lax.fori_loop(0, NX, shard, 0)


def sum_copies_body(gathered, out):
    value = jnp.sum(gathered[...], axis=0)
    for w in range(out.shape[0]):
        out[w] = value


def spread_body(gathered, out):
    for w in range(NX):
        out[w] = gathered[...]


def contract_out_body(gathered, out):
    for x in range(NX):
        for z in range(NZ):
            f, at = z // 2 * 8, x * COLS + z % 2 * WIDE
            out[f : f + 8, at : at + WIDE] = gathered[x, z]


def shards(pool_feat, contract_feat, supply, caps, eligible, grad_log_pool, grad_log_contract):
    x = lax.rem(lax.axis_index("pool"), NX)
    (packed,) = call(
        pack_body,
        [shape(NX, PACK, ROWS_IN)],
        [
            pool_feat.T,
            supply.reshape(1, -1),
            grad_log_pool.reshape(1, -1),
            eligible,
        ],
        smem=(3,),
    )
    packed = over_x(packed)
    cft = lax.dynamic_slice_in_dim(contract_feat.T, x * COLS, COLS, 1)
    demand = lax.dynamic_slice_in_dim(caps.reshape(-1, LANES), x * CG, CG, 0).astype(F32)
    grad_c = lax.dynamic_slice_in_dim(grad_log_contract.reshape(-1, LANES), x * CG, CG, 0)

    acc = pltpu.VMEM((8, COLS), F32)
    col_vec, row_vec = shape(CG, LANES), shape(RG, LANES)
    to_z_both = shape(NZ, CG, WIDE + LANES)
    to_z, to_rows = shape(NZ, CG, LANES), shape(NXC, RG, LANES)
    size = ROWS * COLS

    kern, kern16, a, grad_p, part = call(
        kernel_body,
        [shape(ROWS, COLS), shape(ROWS, COLS, dtype=BF16), row_vec, row_vec, to_z],
        [packed, cft],
        scratch=[acc],
        flops=size * 256,
        trans=size,
    )
    got = over_z(part)
    (ones_part,) = call(
        ones_features_body,
        [shape(NZ, 8, WIDE)],
        [packed, kern16],
        flops=size * 512,
    )
    got, ones_part = lax.optimization_barrier((got, ones_part))
    v1, part = call(
        forward_columns_body, [col_vec, to_rows], [got, demand, kern], flops=2 * size
    )
    got = over_rows(part)
    r1, u1, part = call(
        first_rows_body,
        [row_vec, row_vec, to_z_both],
        [got, a, kern, ones_part],
        scratch=[acc],
        flops=2 * size,
    )
    got = over_z(part)
    (with_u1,) = call(
        features_body, [shape(F, COLS)], [packed, u1, kern16], flops=size * 512
    )
    got, with_u1 = lax.optimization_barrier((got, with_u1))
    v2, ones, part = call(
        first_columns_body,
        [col_vec, shape(8, WIDE), to_rows],
        [got, demand, kern],
        flops=2 * size,
    )
    got = over_rows(part)
    adj2, part = call(
        last_rows_body, [row_vec, to_z], [got, grad_p, kern], scratch=[acc], flops=2 * size
    )
    got = over_z(part)
    (with_adj2,) = call(
        features_body, [shape(F, COLS)], [packed, adj2, kern16], flops=size * 512
    )
    got, with_adj2 = lax.optimization_barrier((got, with_adj2))
    c2, part = call(
        adjoint_columns_body,
        [col_vec, to_rows],
        [got, demand, v2, grad_c, kern],
        flops=2 * size,
    )
    got = over_rows(part)
    adj1, part = call(
        inner_rows_body,
        [row_vec, to_z_both],
        [got, u1, r1, kern, kern16, packed, v1, v2, c2, with_adj2, with_u1],
        scratch=[acc],
        flops=size * 512,
    )
    got = over_z(part)
    c1, owned = call(
        owner_body, [col_vec, shape(NZ, 8, WIDE)], [got, ones, v1, demand]
    )
    contract_got = over_z(owned)
    (pool_part,) = call(
        pool_part_body,
        [shape(NXC, 8, ROWS_IN)],
        [c1, v1, v2, c2, adj2, u1, adj1, kern, cft],
        scratch=[pltpu.VMEM((ROWS_IN, COLS), BF16)],
        flops=size * 512,
    )
    contract_got, pool_part = lax.optimization_barrier((contract_got, pool_part))
    pool_got = over_rows(pool_part)
    (spread,) = call(spread_body, [shape(NX, NZ, 8, WIDE)], [contract_got])
    pool_got, spread = lax.optimization_barrier((pool_got, spread))
    contract_got = over_x(spread)
    (pool_copies,) = call(
        sum_copies_body, [shape(NCON, 8, ROWS_IN)], [pool_got]
    )
    contract_got, pool_copies = lax.optimization_barrier((contract_got, pool_copies))
    pool_got = over_con(pool_copies)
    (contract_grad,) = call(contract_out_body, [shape(F, NX * COLS)], [contract_got])
    return pool_got.reshape(F, ROWS_IN).T, contract_grad.T


def solution(mesh):
    placed = (
        P("pool", None),
        P("con", None),
        P("pool"),
        P("con"),
        P("pool", "con"),
        P("pool"),
        P("con"),
    )
    return jax.shard_map(
        shards,
        mesh=mesh,
        in_specs=placed,
        out_specs=(P("pool", None), P("con", None)),
        check_vma=False,
    )
```

```python
import jax
import jax.numpy as jnp
from jax import lax
from jax.experimental import pallas as pl
from jax.experimental.pallas import tpu as pltpu
from jax.sharding import PartitionSpec as P

NX = 4
NZ = 16
NCON = 8
NXC = NX * NCON
LANES = 128
F = 64
ROWS_IN = 512
ROWS = NX * ROWS_IN
COLS = 1024
RG = ROWS // LANES
CG = COLS // LANES
TILES_IN = ROWS_IN // LANES
MASK_AT = F + 2
PACK = 80
WIDE = 512
F32 = jnp.float32
BF16 = jnp.bfloat16

ALONG_Z = [[z * NX + x for z in range(NZ)] for x in range(NX)]
ALONG_X = [[z * NX + x for x in range(NX)] for z in range(NZ)]
SAME_Z = [[z * NXC + k for k in range(NXC)] for z in range(NZ)]


def over_z(parts):
    return lax.all_to_all(parts, "pool", 0, 0, tiled=True, axis_index_groups=ALONG_Z)


def over_x(parts):
    return lax.all_to_all(parts, "pool", 0, 0, tiled=True, axis_index_groups=ALONG_X)


def over_con(parts):
    return lax.all_to_all(parts, "con", 0, 0, tiled=True)


def over_rows(parts):
    return lax.all_to_all(
        parts, ("pool", "con"), 0, 0, tiled=True, axis_index_groups=SAME_Z
    )


def call(body, outs, args, scratch=(), hbm=(), flops=0, trans=0):
    vmem = pl.BlockSpec(memory_space=pltpu.VMEM)
    nbytes = sum(a.size * a.dtype.itemsize for a in args) + sum(
        o.size * o.dtype.itemsize for o in outs
    )
    return pl.pallas_call(
        body,
        out_shape=outs,
        in_specs=[
            pl.BlockSpec(memory_space=pltpu.HBM) if i in hbm else vmem
            for i in range(len(args))
        ],
        out_specs=[vmem] * len(outs),
        scratch_shapes=list(scratch),
        compiler_params=pltpu.CompilerParams(vmem_limit_bytes=16 * 1024 * 1024),
        cost_estimate=pl.CostEstimate(
            flops=flops, bytes_accessed=nbytes, transcendentals=trans
        ),
    )(
        *(
            pltpu.with_memory_space_constraint(a, pltpu.HBM) if i in hbm else a
            for i, a in enumerate(args)
        )
    )


def shape(*dims, dtype=F32):
    return jax.ShapeDtypeStruct(dims, dtype)


def pack_body(*refs):
    out, sems = refs[4], refs[9]
    copies = [
        pltpu.make_async_copy(refs[i], refs[5 + i], sems.at[i]) for i in range(4)
    ]
    for copy in copies:
        copy.start()
    for copy in copies:
        copy.wait()
    feat_t, supply, grad, eligible = refs[5:9]
    rows = feat_t[...].astype(F32)
    for x in range(NX):
        out[x, :F, :] = rows
        out[x, F : F + 1, :] = supply[...]
        out[x, F + 1 : F + 2, :] = grad[...]
        for k in range(CG):
            for t in range(TILES_IN):
                out[x, MASK_AT + k : MASK_AT + k + 1, t * LANES : (t + 1) * LANES] = (
                    jnp.full((1, LANES), eligible[t, x * CG + k].astype(F32), F32)
                )
        out[x, MASK_AT + CG :, :] = jnp.zeros((PACK - MASK_AT - CG, ROWS_IN), F32)


def put_columns(row, out, copies):
    for k in range(CG):
        piece = row[:, k * LANES : (k + 1) * LANES]
        for w in range(copies):
            out[w, k : k + 1, :] = piece


def kernel_body(packed, cft, kern, kern16, supply, grad, sums, ones, acc):
    width = 256
    acc[...] = jnp.zeros_like(acc)
    for x in range(NX):
        for t in range(TILES_IN):
            at = slice(t * LANES, (t + 1) * LANES)
            g = x * TILES_IN + t
            supply[g : g + 1, :] = packed[x, F : F + 1, at]
            grad[g : g + 1, :] = packed[x, F + 1 : F + 2, at]

    def per_shard(x, _):
        for h in range(2):
            feat = packed[x, :F, h * 256 : h * 256 + 256].T.astype(BF16)
            base = pl.multiple_of(x * ROWS_IN + h * 256, 256)
            for n in range(COLS // width):
                scores = jnp.dot(
                    feat,
                    cft[:, n * width : (n + 1) * width],
                    preferred_element_type=F32,
                )
                values = jnp.exp(scores * 0.125)
                for t in range(2):
                    for j in range(2):
                        k = n * 2 + j
                        tile = h * 2 + t
                        block = (
                            values[t * 128 : t * 128 + 128, j * 128 : j * 128 + 128]
                            * packed[
                                x,
                                MASK_AT + k : MASK_AT + k + 1,
                                tile * 128 : tile * 128 + 128,
                            ]
                        )
                        rows = pl.ds(base + t * 128, 128)
                        kern[rows, k * 128 : k * 128 + 128] = block
                        kern16[rows, k * 128 : k * 128 + 128] = block.astype(BF16)
                        acc[:, k * 128 : k * 128 + 128] += jnp.sum(
                            block.reshape(16, 8, 128), axis=0
                        )
        return 0

    lax.fori_loop(0, NX, per_shard, 0)
    put_columns(jnp.sum(acc[...], axis=0, keepdims=True), sums, NZ)
    feat = jnp.concatenate([packed[x, :F, :] for x in range(NX)], axis=1).astype(BF16)
    put_features(jnp.dot(feat, kern16[...], preferred_element_type=F32), ones)


def row_sums(kern, vec, out, copies):
    def group(g, _):
        rows = pl.ds(pl.multiple_of(g * LANES, LANES), LANES)
        total = kern[rows, 0:LANES] * vec[0:1, :]
        for k in range(1, CG):
            total += kern[rows, k * LANES : (k + 1) * LANES] * vec[k : k + 1, :]
        line = jnp.sum(total.T, axis=0, keepdims=True)
        for w in range(copies):
            out[w, pl.ds(g, 1), :] = line
        return 0

    lax.fori_loop(0, RG, group, 0, unroll=2)


def as_column(vec, g):
    return jnp.broadcast_to(vec[pl.ds(g, 1), :], (LANES, LANES)).T


def column_sums(kern, vec, out, copies, acc):
    acc[...] = jnp.zeros_like(acc)

    def group(g, _):
        rows = pl.ds(pl.multiple_of(g * LANES, LANES), LANES)
        weight = as_column(vec, g)
        for k in range(CG):
            block = kern[rows, k * LANES : (k + 1) * LANES] * weight
            acc[:, k * LANES : (k + 1) * LANES] += jnp.sum(
                block.reshape(16, 8, LANES), axis=0
            )
        return 0

    lax.fori_loop(0, RG, group, 0, unroll=2)
    put_columns(jnp.sum(acc[...], axis=0, keepdims=True), out, copies)


def forward_columns_body(gathered, demand, kern, scale, out):
    scale[...] = demand[...] / jnp.sum(gathered[...], axis=0)
    row_sums(kern, scale, out, NXC)


def second_columns_body(gathered, demand, kern, scale, ones, out):
    ones[...] = jnp.sum(gathered[:, :, :WIDE], axis=0)
    forward_columns_body(gathered.at[:, :, WIDE:], demand, kern, scale, out)


def adjoint_columns_body(gathered, demand, scale, grad, kern, adj, out):
    s = scale[...]
    summed = jnp.sum(gathered[...], axis=0)
    adj[...] = -(grad[...] / s + summed) * s * s / demand[...]
    row_sums(kern, adj, out, NXC)


def split(value):
    high = value.astype(BF16)
    return high, (value - high.astype(F32)).astype(BF16)


def feature_sums(packed, vec, kern16):
    lines = [
        packed[g // TILES_IN, :F, g % TILES_IN * LANES : (g % TILES_IN + 1) * LANES]
        * vec[g : g + 1, :]
        for g in range(RG)
    ]
    high, low = split(jnp.concatenate(lines, axis=1))
    both = jnp.dot(
        jnp.concatenate([high, low], axis=0), kern16[...], preferred_element_type=F32
    )
    return both[:F] + both[F:]


def put_features(value, out):
    for z in range(NZ):
        f, half = z // 2 * 8, z % 2 * WIDE
        out[z] = value[f : f + 8, half : half + WIDE]


def forward_rows_body(
    gathered, supply, kern, kern16, packed, ones, total, scale, features, out, acc
):
    total[...] = jnp.sum(gathered[...], axis=0)
    scale[...] = supply[...] / total[...]
    out[:, :, :WIDE] = ones[...]
    column_sums(kern, scale, out.at[:, :, WIDE:], NZ, acc)
    features[...] = feature_sums(packed, scale, kern16)


def last_rows_body(gathered, grad, kern, kern16, packed, adj, features, out, acc):
    adj[...] = -grad[...] / jnp.sum(gathered[...], axis=0)
    column_sums(kern, adj, out, NZ, acc)
    features[...] = feature_sums(packed, adj, kern16)


def as_row(vec):
    return jnp.concatenate([vec[k : k + 1, :] for k in range(CG)], axis=1)


def inner_rows_body(
    gathered, scale, total, kern, kern16, packed, v1, v2, c2, with_adj2, with_u1, adj, out, acc
):
    adj[...] = -jnp.sum(gathered[...], axis=0) * scale[...] / total[...]
    put_features(
        as_row(v2) * with_adj2[...]
        + as_row(c2) * with_u1[...]
        + as_row(v1) * feature_sums(packed, adj, kern16),
        out.at[:, :, :WIDE],
    )
    column_sums(kern, adj, out.at[:, :, WIDE:], NZ, acc)


def owner_body(gathered, ones, v1, demand, c1, out):
    v = v1[...]
    c1[...] = -jnp.sum(gathered[:, :, WIDE:], axis=0) * v * v / demand[...]
    scale = as_row(c1)
    odd = lax.rem(lax.div(lax.axis_index("pool"), NX), 2) == 1
    mine = jnp.where(odd, scale[:, WIDE:], scale[:, :WIDE]) * ones[...]
    value = (jnp.sum(gathered[:, :, :WIDE], axis=0) + mine) * 0.125
    for w in range(NZ):
        out[w] = value


def pool_part_body(c1, v1, v2, c2, adj2, u1, adj1, kern, cft, out, prod):
    def shard(x, _):
        for t in range(TILES_IN):
            g = x * TILES_IN + t
            rows = pl.ds(pl.multiple_of(g * LANES, LANES), LANES)
            a2, uu, a1 = as_column(adj2, g), as_column(u1, g), as_column(adj1, g)
            for k in range(CG):
                at = slice(k * LANES, (k + 1) * LANES)
                one = slice(k, k + 1)
                w = a2 * v2[one, :] + uu * c2[one, :] + a1 * v1[one, :] + c1[one, :]
                prod[t * LANES : (t + 1) * LANES, at] = (kern[rows, at] * w).astype(BF16)
        part = lax.dot_general(
            cft[...], prod[...], (((1,), (1,)), ((), ())), preferred_element_type=F32
        )
        for c in range(NCON):
            out[x * NCON + c] = part[c * 8 : c * 8 + 8, :] * 0.125
        return 0

    lax.fori_loop(0, NX, shard, 0)


def sum_copies_body(gathered, out):
    value = jnp.sum(gathered[...], axis=0)
    for w in range(out.shape[0]):
        out[w] = value


def spread_body(gathered, out):
    for w in range(NX):
        out[w] = gathered[...]


def contract_out_body(gathered, out):
    for x in range(NX):
        for z in range(NZ):
            f, at = z // 2 * 8, x * COLS + z % 2 * WIDE
            out[f : f + 8, at : at + WIDE] = gathered[x, z]


def shards(pool_feat, contract_feat, supply, caps, eligible, grad_log_pool, grad_log_contract):
    x = lax.rem(lax.axis_index("pool"), NX)
    (packed,) = call(
        pack_body,
        [shape(NX, PACK, ROWS_IN)],
        [
            pool_feat.T,
            supply.reshape(1, -1),
            grad_log_pool.reshape(1, -1),
            eligible,
        ],
        scratch=[
            pltpu.VMEM((F, ROWS_IN), BF16),
            pltpu.VMEM((1, ROWS_IN), F32),
            pltpu.VMEM((1, ROWS_IN), F32),
            pltpu.SMEM((TILES_IN, NX * CG), jnp.int32),
            pltpu.SemaphoreType.DMA((4,)),
        ],
        hbm=(0, 1, 2, 3),
    )
    packed = over_x(packed)
    cft = lax.dynamic_slice_in_dim(contract_feat.T, x * COLS, COLS, 1)
    demand = lax.dynamic_slice_in_dim(caps.reshape(-1, LANES), x * CG, CG, 0).astype(F32)
    grad_c = lax.dynamic_slice_in_dim(grad_log_contract.reshape(-1, LANES), x * CG, CG, 0)

    acc = pltpu.VMEM((8, COLS), F32)
    col_vec, row_vec = shape(CG, LANES), shape(RG, LANES)
    to_z_both = shape(NZ, CG, WIDE + LANES)
    to_z, to_rows = shape(NZ, CG, LANES), shape(NXC, RG, LANES)
    features = shape(F, COLS)
    size = ROWS * COLS

    packed, cft, demand, grad_c = lax.optimization_barrier((packed, cft, demand, grad_c))
    kern, kern16, a, grad_p, part, ones = call(
        kernel_body,
        [
            shape(ROWS, COLS),
            shape(ROWS, COLS, dtype=BF16),
            row_vec,
            row_vec,
            to_z,
            shape(NZ, 8, WIDE),
        ],
        [packed, cft],
        scratch=[acc],
        flops=size * 512,
        trans=size,
    )
    got = over_z(part)
    v1, part = call(
        forward_columns_body, [col_vec, to_rows], [got, demand, kern], flops=2 * size
    )
    got = over_rows(part)
    r1, u1, with_u1, part = call(
        forward_rows_body,
        [row_vec, row_vec, features, to_z_both],
        [got, a, kern, kern16, packed, ones],
        scratch=[acc],
        flops=size * 512,
    )
    got = over_z(part)
    v2, ones, part = call(
        second_columns_body,
        [col_vec, shape(8, WIDE), to_rows],
        [got, demand, kern],
        flops=2 * size,
    )
    got = over_rows(part)
    adj2, with_adj2, part = call(
        last_rows_body,
        [row_vec, features, to_z],
        [got, grad_p, kern, kern16, packed],
        scratch=[acc],
        flops=size * 512,
    )
    got = over_z(part)
    c2, part = call(
        adjoint_columns_body,
        [col_vec, to_rows],
        [got, demand, v2, grad_c, kern],
        flops=2 * size,
    )
    got = over_rows(part)
    adj1, part = call(
        inner_rows_body,
        [row_vec, to_z_both],
        [got, u1, r1, kern, kern16, packed, v1, v2, c2, with_adj2, with_u1],
        scratch=[acc],
        flops=size * 512,
    )
    got = over_z(part)
    c1, owned = call(
        owner_body, [col_vec, shape(NZ, 8, WIDE)], [got, ones, v1, demand]
    )
    contract_got = over_z(owned)
    (pool_part,) = call(
        pool_part_body,
        [shape(NXC, 8, ROWS_IN)],
        [c1, v1, v2, c2, adj2, u1, adj1, kern, cft],
        scratch=[pltpu.VMEM((ROWS_IN, COLS), BF16)],
        flops=size * 512,
    )
    contract_got, pool_part = lax.optimization_barrier((contract_got, pool_part))
    pool_got = over_rows(pool_part)
    (spread,) = call(spread_body, [shape(NX, NZ, 8, WIDE)], [contract_got])
    pool_got, spread = lax.optimization_barrier((pool_got, spread))
    contract_got = over_x(spread)
    (pool_copies,) = call(
        sum_copies_body, [shape(NCON, 8, ROWS_IN)], [pool_got]
    )
    contract_got, pool_copies = lax.optimization_barrier((contract_got, pool_copies))
    pool_got = over_con(pool_copies)
    (contract_grad,) = call(contract_out_body, [shape(F, NX * COLS)], [contract_got])
    return pool_got.reshape(F, ROWS_IN).T, contract_grad.T


def solution(mesh):
    placed = (
        P("pool", None),
        P("con", None),
        P("pool"),
        P("con"),
        P("pool", "con"),
        P("pool"),
        P("con"),
    )
    return jax.shard_map(
        shards,
        mesh=mesh,
        in_specs=placed,
        out_specs=(P("pool", None), P("con", None)),
        check_vma=False,
    )
```

```python
import jax
import jax.numpy as jnp
from jax import lax
from jax.experimental import pallas as pl
from jax.experimental.pallas import tpu as pltpu
from jax.sharding import PartitionSpec as P

NX = 4
NZ = 16
NCON = 8
NXC = NX * NCON
LANES = 128
F = 64
ROWS_IN = 512
ROWS = NX * ROWS_IN
COLS = 1024
RG = ROWS // LANES
CG = COLS // LANES
TILES_IN = ROWS_IN // LANES
MASK_AT = F + 2
PACK = 80
WIDE = 512
F32 = jnp.float32
BF16 = jnp.bfloat16

ALONG_Z = [[z * NX + x for z in range(NZ)] for x in range(NX)]
ALONG_X = [[z * NX + x for x in range(NX)] for z in range(NZ)]
SAME_Z = [[z * NXC + k for k in range(NXC)] for z in range(NZ)]


def over_z(parts):
    return lax.all_to_all(parts, "pool", 0, 0, tiled=True, axis_index_groups=ALONG_Z)


def over_x(parts):
    return lax.all_to_all(parts, "pool", 0, 0, tiled=True, axis_index_groups=ALONG_X)


def to_next_x(part, step):
    moves = [
        (z * NX + x, z * NX + (x + step) % NX) for z in range(NZ) for x in range(NX)
    ]
    return lax.ppermute(part, "pool", moves)


def over_con(parts):
    return lax.all_to_all(parts, "con", 0, 0, tiled=True)


def over_rows(parts):
    return lax.all_to_all(
        parts, ("pool", "con"), 0, 0, tiled=True, axis_index_groups=SAME_Z
    )


def call(body, outs, args, scratch=(), hbm=(), flops=0, trans=0):
    vmem = pl.BlockSpec(memory_space=pltpu.VMEM)
    nbytes = sum(a.size * a.dtype.itemsize for a in args) + sum(
        o.size * o.dtype.itemsize for o in outs
    )
    return pl.pallas_call(
        body,
        out_shape=outs,
        in_specs=[
            pl.BlockSpec(memory_space=pltpu.HBM) if i in hbm else vmem
            for i in range(len(args))
        ],
        out_specs=[vmem] * len(outs),
        scratch_shapes=list(scratch),
        compiler_params=pltpu.CompilerParams(vmem_limit_bytes=16 * 1024 * 1024),
        cost_estimate=pl.CostEstimate(
            flops=flops, bytes_accessed=nbytes, transcendentals=trans
        ),
    )(
        *(
            pltpu.with_memory_space_constraint(a, pltpu.HBM) if i in hbm else a
            for i, a in enumerate(args)
        )
    )


def shape(*dims, dtype=F32):
    return jax.ShapeDtypeStruct(dims, dtype)


def pack_body(*refs):
    out, sems = refs[4], refs[9]
    copies = [
        pltpu.make_async_copy(refs[i], refs[5 + i], sems.at[i]) for i in range(4)
    ]
    for copy in copies:
        copy.start()
    for copy in copies:
        copy.wait()
    feat_t, supply, grad, eligible = refs[5:9]
    rows = feat_t[...].astype(F32)
    for x in range(NX):
        out[x, :F, :] = rows
        out[x, F : F + 1, :] = supply[...]
        out[x, F + 1 : F + 2, :] = grad[...]
        for k in range(CG):
            for t in range(TILES_IN):
                out[x, MASK_AT + k : MASK_AT + k + 1, t * LANES : (t + 1) * LANES] = (
                    jnp.full((1, LANES), eligible[t, x * CG + k].astype(F32), F32)
                )
        out[x, MASK_AT + CG :, :] = jnp.zeros((PACK - MASK_AT - CG, ROWS_IN), F32)


def put_columns(row, out, copies):
    for k in range(CG):
        piece = row[:, k * LANES : (k + 1) * LANES]
        for w in range(copies):
            out[w, k : k + 1, :] = piece


def kernel_body(packed, cft, kern, kern16, supply, grad, sums, ones, acc):
    width = 256
    acc[...] = jnp.zeros_like(acc)
    for x in range(NX):
        for t in range(TILES_IN):
            at = slice(t * LANES, (t + 1) * LANES)
            g = x * TILES_IN + t
            supply[g : g + 1, :] = packed[x, F : F + 1, at]
            grad[g : g + 1, :] = packed[x, F + 1 : F + 2, at]

    def per_shard(x, _):
        for h in range(2):
            feat = packed[x, :F, h * 256 : h * 256 + 256].T.astype(BF16)
            base = pl.multiple_of(x * ROWS_IN + h * 256, 256)
            for n in range(COLS // width):
                scores = jnp.dot(
                    feat,
                    cft[:, n * width : (n + 1) * width],
                    preferred_element_type=F32,
                )
                values = jnp.exp(scores * 0.125)
                for t in range(2):
                    for j in range(2):
                        k = n * 2 + j
                        tile = h * 2 + t
                        block = (
                            values[t * 128 : t * 128 + 128, j * 128 : j * 128 + 128]
                            * packed[
                                x,
                                MASK_AT + k : MASK_AT + k + 1,
                                tile * 128 : tile * 128 + 128,
                            ]
                        )
                        rows = pl.ds(base + t * 128, 128)
                        kern[rows, k * 128 : k * 128 + 128] = block
                        kern16[rows, k * 128 : k * 128 + 128] = block.astype(BF16)
                        acc[:, k * 128 : k * 128 + 128] += jnp.sum(
                            block.reshape(16, 8, 128), axis=0
                        )
        return 0

    lax.fori_loop(0, NX, per_shard, 0)
    put_columns(jnp.sum(acc[...], axis=0, keepdims=True), sums, NZ)
    feat = jnp.concatenate([packed[x, :F, :] for x in range(NX)], axis=1).astype(BF16)
    put_features(jnp.dot(feat, kern16[...], preferred_element_type=F32), ones)


def row_sums(kern, vec, out, copies):
    def group(g, _):
        rows = pl.ds(pl.multiple_of(g * LANES, LANES), LANES)
        total = kern[rows, 0:LANES] * vec[0:1, :]
        for k in range(1, CG):
            total += kern[rows, k * LANES : (k + 1) * LANES] * vec[k : k + 1, :]
        line = jnp.sum(total.T, axis=0, keepdims=True)
        for w in range(copies):
            out[w, pl.ds(g, 1), :] = line
        return 0

    lax.fori_loop(0, RG, group, 0, unroll=2)


def as_column(vec, g):
    return jnp.broadcast_to(vec[pl.ds(g, 1), :], (LANES, LANES)).T


def column_sums(kern, vec, out, copies, acc):
    acc[...] = jnp.zeros_like(acc)

    def group(g, _):
        rows = pl.ds(pl.multiple_of(g * LANES, LANES), LANES)
        weight = as_column(vec, g)
        for k in range(CG):
            block = kern[rows, k * LANES : (k + 1) * LANES] * weight
            acc[:, k * LANES : (k + 1) * LANES] += jnp.sum(
                block.reshape(16, 8, LANES), axis=0
            )
        return 0

    lax.fori_loop(0, RG, group, 0, unroll=2)
    put_columns(jnp.sum(acc[...], axis=0, keepdims=True), out, copies)


def forward_columns_body(gathered, demand, kern, scale, out):
    scale[...] = demand[...] / jnp.sum(gathered[...], axis=0)
    row_sums(kern, scale, out, NXC)


def second_columns_body(gathered, demand, kern, scale, ones, out):
    ones[...] = jnp.sum(gathered[:, :, :WIDE], axis=0)
    forward_columns_body(gathered.at[:, :, WIDE:], demand, kern, scale, out)


def adjoint_columns_body(gathered, demand, scale, grad, kern, adj, out):
    s = scale[...]
    summed = jnp.sum(gathered[...], axis=0)
    adj[...] = -(grad[...] / s + summed) * s * s / demand[...]
    row_sums(kern, adj, out, NXC)


def split(value):
    high = value.astype(BF16)
    return high, (value - high.astype(F32)).astype(BF16)


def feature_sums(packed, vec, kern16):
    lines = [
        packed[g // TILES_IN, :F, g % TILES_IN * LANES : (g % TILES_IN + 1) * LANES]
        * vec[g : g + 1, :]
        for g in range(RG)
    ]
    high, low = split(jnp.concatenate(lines, axis=1))
    both = jnp.dot(
        jnp.concatenate([high, low], axis=0), kern16[...], preferred_element_type=F32
    )
    return both[:F] + both[F:]


def put_features(value, out):
    for z in range(NZ):
        f, half = z // 2 * 8, z % 2 * WIDE
        out[z] = value[f : f + 8, half : half + WIDE]


def forward_rows_body(
    gathered, supply, kern, kern16, packed, ones, total, scale, features, out, acc
):
    total[...] = jnp.sum(gathered[...], axis=0)
    scale[...] = supply[...] / total[...]
    out[:, :, :WIDE] = ones[...]
    column_sums(kern, scale, out.at[:, :, WIDE:], NZ, acc)
    features[...] = feature_sums(packed, scale, kern16)


def last_rows_body(gathered, grad, kern, kern16, packed, adj, features, out, acc):
    adj[...] = -grad[...] / jnp.sum(gathered[...], axis=0)
    column_sums(kern, adj, out, NZ, acc)
    features[...] = feature_sums(packed, adj, kern16)


def as_row(vec):
    return jnp.concatenate([vec[k : k + 1, :] for k in range(CG)], axis=1)


def inner_rows_body(
    gathered, scale, total, kern, kern16, packed, v1, v2, c2, with_adj2, with_u1, adj, out, acc
):
    adj[...] = -jnp.sum(gathered[...], axis=0) * scale[...] / total[...]
    put_features(
        as_row(v2) * with_adj2[...]
        + as_row(c2) * with_u1[...]
        + as_row(v1) * feature_sums(packed, adj, kern16),
        out.at[:, :, :WIDE],
    )
    column_sums(kern, adj, out.at[:, :, WIDE:], NZ, acc)


def owner_body(gathered, ones, v1, demand, c1, out):
    v = v1[...]
    c1[...] = -jnp.sum(gathered[:, :, WIDE:], axis=0) * v * v / demand[...]
    scale = as_row(c1)
    odd = lax.rem(lax.div(lax.axis_index("pool"), NX), 2) == 1
    mine = jnp.where(odd, scale[:, WIDE:], scale[:, :WIDE]) * ones[...]
    value = (jnp.sum(gathered[:, :, :WIDE], axis=0) + mine) * 0.125
    for w in range(NZ):
        out[w] = value


def pool_part_body(c1, v1, v2, c2, adj2, u1, adj1, kern, cft, out, prod):
    def shard(x, _):
        for t in range(TILES_IN):
            g = x * TILES_IN + t
            rows = pl.ds(pl.multiple_of(g * LANES, LANES), LANES)
            a2, uu, a1 = as_column(adj2, g), as_column(u1, g), as_column(adj1, g)
            for k in range(CG):
                at = slice(k * LANES, (k + 1) * LANES)
                one = slice(k, k + 1)
                w = a2 * v2[one, :] + uu * c2[one, :] + a1 * v1[one, :] + c1[one, :]
                prod[t * LANES : (t + 1) * LANES, at] = (kern[rows, at] * w).astype(BF16)
        part = lax.dot_general(
            cft[...], prod[...], (((1,), (1,)), ((), ())), preferred_element_type=F32
        )
        for c in range(NCON):
            out[x * NCON + c] = part[c * 8 : c * 8 + 8, :] * 0.125
        return 0

    lax.fori_loop(0, NX, shard, 0)


def sum_copies_body(gathered, out):
    value = jnp.sum(gathered[...], axis=0)
    for w in range(out.shape[0]):
        out[w] = value


def contract_out_body(own, before, after, far_low, far_high, out):
    x = lax.rem(lax.axis_index("pool"), NX)

    def put(part, shift, first):
        base = lax.rem(x + shift, NX) * COLS
        for i in range(part.shape[0]):
            z = first + i
            at = pl.ds(pl.multiple_of(base + z % 2 * WIDE, WIDE), WIDE)
            out[z // 2 * 8 : z // 2 * 8 + 8, at] = part[i]

    put(own, 0, 0)
    put(before, NX - 1, 0)
    put(after, 1, 0)
    put(far_low, NX // 2, 0)
    put(far_high, NX // 2, NZ // 2)


def shards(pool_feat, contract_feat, supply, caps, eligible, grad_log_pool, grad_log_contract):
    x = lax.rem(lax.axis_index("pool"), NX)
    (packed,) = call(
        pack_body,
        [shape(NX, PACK, ROWS_IN)],
        [
            pool_feat.T,
            supply.reshape(1, -1),
            grad_log_pool.reshape(1, -1),
            eligible,
        ],
        scratch=[
            pltpu.VMEM((F, ROWS_IN), BF16),
            pltpu.VMEM((1, ROWS_IN), F32),
            pltpu.VMEM((1, ROWS_IN), F32),
            pltpu.SMEM((TILES_IN, NX * CG), jnp.int32),
            pltpu.SemaphoreType.DMA((4,)),
        ],
        hbm=(0, 1, 2, 3),
    )
    packed = over_x(packed)
    cft = lax.dynamic_slice_in_dim(contract_feat.T, x * COLS, COLS, 1)
    demand = lax.dynamic_slice_in_dim(caps.reshape(-1, LANES), x * CG, CG, 0).astype(F32)
    grad_c = lax.dynamic_slice_in_dim(grad_log_contract.reshape(-1, LANES), x * CG, CG, 0)

    acc = pltpu.VMEM((8, COLS), F32)
    col_vec, row_vec = shape(CG, LANES), shape(RG, LANES)
    to_z_both = shape(NZ, CG, WIDE + LANES)
    to_z, to_rows = shape(NZ, CG, LANES), shape(NXC, RG, LANES)
    features = shape(F, COLS)
    size = ROWS * COLS

    packed, cft, demand, grad_c = lax.optimization_barrier((packed, cft, demand, grad_c))
    kern, kern16, a, grad_p, part, ones = call(
        kernel_body,
        [
            shape(ROWS, COLS),
            shape(ROWS, COLS, dtype=BF16),
            row_vec,
            row_vec,
            to_z,
            shape(NZ, 8, WIDE),
        ],
        [packed, cft],
        scratch=[acc],
        flops=size * 512,
        trans=size,
    )
    got = over_z(part)
    v1, part = call(
        forward_columns_body, [col_vec, to_rows], [got, demand, kern], flops=2 * size
    )
    got = over_rows(part)
    r1, u1, with_u1, part = call(
        forward_rows_body,
        [row_vec, row_vec, features, to_z_both],
        [got, a, kern, kern16, packed, ones],
        scratch=[acc],
        flops=size * 512,
    )
    got = over_z(part)
    v2, ones, part = call(
        second_columns_body,
        [col_vec, shape(8, WIDE), to_rows],
        [got, demand, kern],
        flops=2 * size,
    )
    got = over_rows(part)
    adj2, with_adj2, part = call(
        last_rows_body,
        [row_vec, features, to_z],
        [got, grad_p, kern, kern16, packed],
        scratch=[acc],
        flops=size * 512,
    )
    got = over_z(part)
    c2, part = call(
        adjoint_columns_body,
        [col_vec, to_rows],
        [got, demand, v2, grad_c, kern],
        flops=2 * size,
    )
    got = over_rows(part)
    adj1, part = call(
        inner_rows_body,
        [row_vec, to_z_both],
        [got, u1, r1, kern, kern16, packed, v1, v2, c2, with_adj2, with_u1],
        scratch=[acc],
        flops=size * 512,
    )
    got = over_z(part)
    c1, owned = call(
        owner_body, [col_vec, shape(NZ, 8, WIDE)], [got, ones, v1, demand]
    )
    contract_got = over_z(owned)
    (pool_part,) = call(
        pool_part_body,
        [shape(NXC, 8, ROWS_IN)],
        [c1, v1, v2, c2, adj2, u1, adj1, kern, cft],
        scratch=[pltpu.VMEM((ROWS_IN, COLS), BF16)],
        flops=size * 512,
    )
    contract_got, pool_part = lax.optimization_barrier((contract_got, pool_part))
    pool_got = over_rows(pool_part)
    before, after = to_next_x(contract_got, 1), to_next_x(contract_got, -1)
    far_low = to_next_x(before[: NZ // 2], 1)
    far_high = to_next_x(after[NZ // 2 :], -1)
    (pool_copies,) = call(
        sum_copies_body, [shape(NCON, 8, ROWS_IN)], [pool_got]
    )
    pool_got = over_con(pool_copies)
    (contract_grad,) = call(
        contract_out_body,
        [shape(F, NX * COLS)],
        [contract_got, before, after, far_low, far_high],
    )
    return pool_got.reshape(F, ROWS_IN).T, contract_grad.T


def solution(mesh):
    placed = (
        P("pool", None),
        P("con", None),
        P("pool"),
        P("con"),
        P("pool", "con"),
        P("pool"),
        P("con"),
    )
    return jax.shard_map(
        shards,
        mesh=mesh,
        in_specs=placed,
        out_specs=(P("pool", None), P("con", None)),
        check_vma=False,
    )
```

```python
import math

import jax
import jax.numpy as jnp
from jax import lax
from jax.experimental import pallas as pl
from jax.experimental.pallas import tpu as pltpu
from jax.sharding import PartitionSpec as P

NX = 4
NZ = 16
NCON = 8
NXC = NX * NCON
LANES = 128
F = 64
ROWS_IN = 512
ROWS = NX * ROWS_IN
COLS = 1024
RG = ROWS // LANES
CG = COLS // LANES
TILES_IN = ROWS_IN // LANES
MASK_AT = F + 2
PACK = 80
WIDE = 512
EXPONENT = 0.125 * math.log2(math.e)
F32 = jnp.float32
BF16 = jnp.bfloat16

ALONG_Z = [[z * NX + x for z in range(NZ)] for x in range(NX)]
ALONG_X = [[z * NX + x for x in range(NX)] for z in range(NZ)]
SAME_Z = [[z * NXC + k for k in range(NXC)] for z in range(NZ)]


def over_z(parts):
    return lax.all_to_all(parts, "pool", 0, 0, tiled=True, axis_index_groups=ALONG_Z)


def over_x(parts):
    return lax.all_to_all(parts, "pool", 0, 0, tiled=True, axis_index_groups=ALONG_X)


def to_next_x(part, step):
    moves = [
        (z * NX + x, z * NX + (x + step) % NX) for z in range(NZ) for x in range(NX)
    ]
    return lax.ppermute(part, "pool", moves)


def over_con(parts):
    return lax.all_to_all(parts, "con", 0, 0, tiled=True)


def over_rows(parts):
    return lax.all_to_all(
        parts, ("pool", "con"), 0, 0, tiled=True, axis_index_groups=SAME_Z
    )


def call(body, outs, args, scratch=(), hbm=(), flops=0, trans=0):
    vmem = pl.BlockSpec(memory_space=pltpu.VMEM)
    nbytes = sum(a.size * a.dtype.itemsize for a in args) + sum(
        o.size * o.dtype.itemsize for o in outs
    )
    return pl.pallas_call(
        body,
        out_shape=outs,
        in_specs=[
            pl.BlockSpec(memory_space=pltpu.HBM) if i in hbm else vmem
            for i in range(len(args))
        ],
        out_specs=[vmem] * len(outs),
        scratch_shapes=list(scratch),
        compiler_params=pltpu.CompilerParams(vmem_limit_bytes=16 * 1024 * 1024),
        cost_estimate=pl.CostEstimate(
            flops=flops, bytes_accessed=nbytes, transcendentals=trans
        ),
    )(
        *(
            pltpu.with_memory_space_constraint(a, pltpu.HBM) if i in hbm else a
            for i, a in enumerate(args)
        )
    )


def shape(*dims, dtype=F32):
    return jax.ShapeDtypeStruct(dims, dtype)


def pack_body(*refs):
    out, sems = refs[4], refs[9]
    copies = [
        pltpu.make_async_copy(refs[i], refs[5 + i], sems.at[i]) for i in range(4)
    ]
    for copy in copies:
        copy.start()
    for copy in copies:
        copy.wait()
    feat_t, supply, grad, eligible = refs[5:9]
    rows = feat_t[...].astype(F32)
    for x in range(NX):
        out[x, :F, :] = rows
        out[x, F : F + 1, :] = supply[...]
        out[x, F + 1 : F + 2, :] = grad[...]
        for k in range(CG):
            for t in range(TILES_IN):
                out[x, MASK_AT + k : MASK_AT + k + 1, t * LANES : (t + 1) * LANES] = (
                    jnp.full((1, LANES), eligible[t, x * CG + k].astype(F32), F32)
                )
        out[x, MASK_AT + CG :, :] = jnp.zeros((PACK - MASK_AT - CG, ROWS_IN), F32)


def put_columns(row, out, copies):
    for k in range(CG):
        piece = row[:, k * LANES : (k + 1) * LANES]
        for w in range(copies):
            out[w, k : k + 1, :] = piece


def kernel_body(packed, cft, kern, kern16, supply, grad, sums, ones, acc):
    width = 256
    acc[...] = jnp.zeros_like(acc)
    for x in range(NX):
        for t in range(TILES_IN):
            at = slice(t * LANES, (t + 1) * LANES)
            g = x * TILES_IN + t
            supply[g : g + 1, :] = packed[x, F : F + 1, at]
            grad[g : g + 1, :] = packed[x, F + 1 : F + 2, at]

    def per_shard(x, _):
        for h in range(2):
            feat = packed[x, :F, h * 256 : h * 256 + 256].T.astype(BF16)
            base = pl.multiple_of(x * ROWS_IN + h * 256, 256)
            for n in range(COLS // width):
                scores = jnp.dot(
                    feat,
                    cft[:, n * width : (n + 1) * width],
                    preferred_element_type=F32,
                )
                values = jnp.exp2(scores * EXPONENT)
                for t in range(2):
                    for j in range(2):
                        k = n * 2 + j
                        tile = h * 2 + t
                        block = (
                            values[t * 128 : t * 128 + 128, j * 128 : j * 128 + 128]
                            * packed[
                                x,
                                MASK_AT + k : MASK_AT + k + 1,
                                tile * 128 : tile * 128 + 128,
                            ]
                        )
                        rows = pl.ds(base + t * 128, 128)
                        kern[rows, k * 128 : k * 128 + 128] = block
                        kern16[rows, k * 128 : k * 128 + 128] = block.astype(BF16)
                        acc[:, k * 128 : k * 128 + 128] += jnp.sum(
                            block.reshape(16, 8, 128), axis=0
                        )
        return 0

    lax.fori_loop(0, NX, per_shard, 0, unroll=4)
    put_columns(jnp.sum(acc[...], axis=0, keepdims=True), sums, NZ)
    feat = jnp.concatenate([packed[x, :F, :] for x in range(NX)], axis=1).astype(BF16)
    put_features(jnp.dot(feat, kern16[...], preferred_element_type=F32), ones)


def row_sums(kern, vec, out, copies):
    def group(g, _):
        rows = pl.ds(pl.multiple_of(g * LANES, LANES), LANES)
        total = kern[rows, 0:LANES] * vec[0:1, :]
        for k in range(1, CG):
            total += kern[rows, k * LANES : (k + 1) * LANES] * vec[k : k + 1, :]
        line = jnp.sum(total.T, axis=0, keepdims=True)
        for w in range(copies):
            out[w, pl.ds(g, 1), :] = line
        return 0

    lax.fori_loop(0, RG, group, 0, unroll=True)


def as_column(vec, g):
    return jnp.broadcast_to(vec[pl.ds(g, 1), :], (LANES, LANES)).T


def column_sums(kern, vec, out, copies):
    totals = [jnp.zeros((8, LANES), F32)] * CG
    for g in range(RG):
        rows = slice(g * LANES, (g + 1) * LANES)
        weight = as_column(vec, g)
        for k in range(CG):
            block = kern[rows, k * LANES : (k + 1) * LANES] * weight
            totals[k] += jnp.sum(block.reshape(16, 8, LANES), axis=0)
    line = jnp.concatenate(
        [jnp.sum(total, axis=0, keepdims=True) for total in totals], axis=1
    )
    put_columns(line, out, copies)


def forward_columns_body(gathered, demand, kern, scale, out):
    scale[...] = demand[...] / jnp.sum(gathered[...], axis=0)
    row_sums(kern, scale, out, NXC)


def second_columns_body(gathered, demand, kern, scale, ones, out):
    ones[...] = jnp.sum(gathered[:, :, :WIDE], axis=0)
    forward_columns_body(gathered.at[:, :, WIDE:], demand, kern, scale, out)


def adjoint_columns_body(gathered, demand, scale, grad, kern, adj, out):
    s = scale[...]
    summed = jnp.sum(gathered[...], axis=0)
    adj[...] = -(grad[...] / s + summed) * s * s / demand[...]
    row_sums(kern, adj, out, NXC)


def split(value):
    high = value.astype(BF16)
    return high, (value - high.astype(F32)).astype(BF16)


def feature_sums(packed, vecs, kern16):
    halves = []
    for vec in vecs:
        lines = [
            packed[g // TILES_IN, :F, g % TILES_IN * LANES : (g % TILES_IN + 1) * LANES]
            * vec[g : g + 1, :]
            for g in range(RG)
        ]
        halves += split(jnp.concatenate(lines, axis=1))
    sums = jnp.dot(
        jnp.concatenate(halves, axis=0), kern16[...], preferred_element_type=F32
    )
    return [
        sums[i * 2 * F : (i * 2 + 1) * F] + sums[(i * 2 + 1) * F : (i * 2 + 2) * F]
        for i in range(len(vecs))
    ]


def put_features(value, out):
    for z in range(NZ):
        f, half = z // 2 * 8, z % 2 * WIDE
        out[z] = value[f : f + 8, half : half + WIDE]


def forward_rows_body(
    gathered, supply, kern, ones, total, scale, out
):
    total[...] = jnp.sum(gathered[...], axis=0)
    scale[...] = supply[...] / total[...]
    out[:, :, :WIDE] = ones[...]
    column_sums(kern, scale, out.at[:, :, WIDE:], NZ)


def last_rows_body(gathered, grad, kern, adj, out):
    adj[...] = -grad[...] / jnp.sum(gathered[...], axis=0)
    column_sums(kern, adj, out, NZ)


def as_row(vec):
    return jnp.concatenate([vec[k : k + 1, :] for k in range(CG)], axis=1)


def inner_rows_body(
    gathered, scale, total, kern, kern16, packed, v1, v2, c2, adj2, adj, out
):
    adj[...] = -jnp.sum(gathered[...], axis=0) * scale[...] / total[...]
    with_adj2, with_scale, with_adj = feature_sums(packed, [adj2, scale, adj], kern16)
    put_features(
        as_row(v2) * with_adj2 + as_row(c2) * with_scale + as_row(v1) * with_adj,
        out.at[:, :, :WIDE],
    )
    column_sums(kern, adj, out.at[:, :, WIDE:], NZ)


def owner_body(gathered, ones, v1, demand, c1, out):
    v = v1[...]
    c1[...] = -jnp.sum(gathered[:, :, WIDE:], axis=0) * v * v / demand[...]
    scale = as_row(c1)
    odd = lax.rem(lax.div(lax.axis_index("pool"), NX), 2) == 1
    mine = jnp.where(odd, scale[:, WIDE:], scale[:, :WIDE]) * ones[...]
    value = (jnp.sum(gathered[:, :, :WIDE], axis=0) + mine) * 0.125
    for w in range(NZ):
        out[w] = value


def pool_part_body(c1, v1, v2, c2, adj2, u1, adj1, kern, cft, out, prod):
    def shard(x, _):
        for t in range(TILES_IN):
            g = x * TILES_IN + t
            rows = pl.ds(pl.multiple_of(g * LANES, LANES), LANES)
            a2, uu, a1 = as_column(adj2, g), as_column(u1, g), as_column(adj1, g)
            for k in range(CG):
                at = slice(k * LANES, (k + 1) * LANES)
                one = slice(k, k + 1)
                w = a2 * v2[one, :] + uu * c2[one, :] + a1 * v1[one, :] + c1[one, :]
                prod[t * LANES : (t + 1) * LANES, at] = (kern[rows, at] * w).astype(BF16)
        part = lax.dot_general(
            cft[...], prod[...], (((1,), (1,)), ((), ())), preferred_element_type=F32
        )
        for c in range(NCON):
            out[x * NCON + c] = part[c * 8 : c * 8 + 8, :] * 0.125
        return 0

    lax.fori_loop(0, NX, shard, 0)


def sum_copies_body(gathered, out):
    value = jnp.sum(gathered[...], axis=0)
    for w in range(out.shape[0]):
        out[w] = value


def contract_out_body(own, before, after, far_low, far_high, out):
    x = lax.rem(lax.axis_index("pool"), NX)

    def put(part, shift, first):
        base = lax.rem(x + shift, NX) * COLS
        for i in range(part.shape[0]):
            z = first + i
            at = pl.ds(pl.multiple_of(base + z % 2 * WIDE, WIDE), WIDE)
            out[z // 2 * 8 : z // 2 * 8 + 8, at] = part[i]

    put(own, 0, 0)
    put(before, NX - 1, 0)
    put(after, 1, 0)
    put(far_low, NX // 2, 0)
    put(far_high, NX // 2, NZ // 2)


def shards(pool_feat, contract_feat, supply, caps, eligible, grad_log_pool, grad_log_contract):
    x = lax.rem(lax.axis_index("pool"), NX)
    (packed,) = call(
        pack_body,
        [shape(NX, PACK, ROWS_IN)],
        [
            pool_feat.T,
            supply.reshape(1, -1),
            grad_log_pool.reshape(1, -1),
            eligible,
        ],
        scratch=[
            pltpu.VMEM((F, ROWS_IN), BF16),
            pltpu.VMEM((1, ROWS_IN), F32),
            pltpu.VMEM((1, ROWS_IN), F32),
            pltpu.SMEM((TILES_IN, NX * CG), jnp.int32),
            pltpu.SemaphoreType.DMA((4,)),
        ],
        hbm=(0, 1, 2, 3),
    )
    packed = over_x(packed)
    cft = lax.dynamic_slice_in_dim(contract_feat.T, x * COLS, COLS, 1)
    demand = lax.dynamic_slice_in_dim(caps.reshape(-1, LANES), x * CG, CG, 0).astype(F32)
    grad_c = lax.dynamic_slice_in_dim(grad_log_contract.reshape(-1, LANES), x * CG, CG, 0)

    acc = pltpu.VMEM((8, COLS), F32)
    col_vec, row_vec = shape(CG, LANES), shape(RG, LANES)
    to_z_both = shape(NZ, CG, WIDE + LANES)
    to_z, to_rows = shape(NZ, CG, LANES), shape(NXC, RG, LANES)
    size = ROWS * COLS

    packed, cft, demand, grad_c = lax.optimization_barrier((packed, cft, demand, grad_c))
    kern, kern16, a, grad_p, part, ones = call(
        kernel_body,
        [
            shape(ROWS, COLS),
            shape(ROWS, COLS, dtype=BF16),
            row_vec,
            row_vec,
            to_z,
            shape(NZ, 8, WIDE),
        ],
        [packed, cft],
        scratch=[acc],
        flops=size * 512,
        trans=size,
    )
    got = over_z(part)
    v1, part = call(
        forward_columns_body, [col_vec, to_rows], [got, demand, kern], flops=2 * size
    )
    got = over_rows(part)
    r1, u1, part = call(
        forward_rows_body,
        [row_vec, row_vec, to_z_both],
        [got, a, kern, ones],
        flops=2 * size,
    )
    got = over_z(part)
    v2, ones, part = call(
        second_columns_body,
        [col_vec, shape(8, WIDE), to_rows],
        [got, demand, kern],
        flops=2 * size,
    )
    got = over_rows(part)
    adj2, part = call(
        last_rows_body, [row_vec, to_z], [got, grad_p, kern], flops=2 * size
    )
    got = over_z(part)
    c2, part = call(
        adjoint_columns_body,
        [col_vec, to_rows],
        [got, demand, v2, grad_c, kern],
        flops=2 * size,
    )
    got = over_rows(part)
    adj1, part = call(
        inner_rows_body,
        [row_vec, to_z_both],
        [got, u1, r1, kern, kern16, packed, v1, v2, c2, adj2],
        flops=size * 512,
    )
    got = over_z(part)
    c1, owned = call(
        owner_body, [col_vec, shape(NZ, 8, WIDE)], [got, ones, v1, demand]
    )
    contract_got = over_z(owned)
    (pool_part,) = call(
        pool_part_body,
        [shape(NXC, 8, ROWS_IN)],
        [c1, v1, v2, c2, adj2, u1, adj1, kern, cft],
        scratch=[pltpu.VMEM((ROWS_IN, COLS), BF16)],
        flops=size * 512,
    )
    contract_got, pool_part = lax.optimization_barrier((contract_got, pool_part))
    pool_got = over_rows(pool_part)
    before, after = to_next_x(contract_got, 1), to_next_x(contract_got, -1)
    far_low = to_next_x(before[: NZ // 2], 1)
    far_high = to_next_x(after[NZ // 2 :], -1)
    (pool_copies,) = call(
        sum_copies_body, [shape(NCON, 8, ROWS_IN)], [pool_got]
    )
    pool_got = over_con(pool_copies)
    (contract_grad,) = call(
        contract_out_body,
        [shape(F, NX * COLS)],
        [contract_got, before, after, far_low, far_high],
    )
    return pool_got.reshape(F, ROWS_IN).T, contract_grad.T


def solution(mesh):
    placed = (
        P("pool", None),
        P("con", None),
        P("pool"),
        P("con"),
        P("pool", "con"),
        P("pool"),
        P("con"),
    )
    return jax.shard_map(
        shards,
        mesh=mesh,
        in_specs=placed,
        out_specs=(P("pool", None), P("con", None)),
        check_vma=False,
    )
```

```python
import math

import jax
import jax.numpy as jnp
from jax import lax
from jax.experimental import pallas as pl
from jax.experimental.pallas import tpu as pltpu
from jax.sharding import PartitionSpec as P

NX = 4
NZ = 16
NCON = 8
NXC = NX * NCON
LANES = 128
F = 64
ROWS_IN = 512
ROWS = NX * ROWS_IN
COLS = 1024
RG = ROWS // LANES
CG = COLS // LANES
TILES_IN = ROWS_IN // LANES
MASK_AT = F + 2
PACK = 80
WIDE = 512
EXPONENT = 0.125 * math.log2(math.e)
F32 = jnp.float32
BF16 = jnp.bfloat16

ALONG_Z = [[z * NX + x for z in range(NZ)] for x in range(NX)]
ALONG_X = [[z * NX + x for x in range(NX)] for z in range(NZ)]
SAME_Z = [[z * NXC + k for k in range(NXC)] for z in range(NZ)]


def over_z(parts):
    return lax.all_to_all(parts, "pool", 0, 0, tiled=True, axis_index_groups=ALONG_Z)


def over_x(parts):
    return lax.all_to_all(parts, "pool", 0, 0, tiled=True, axis_index_groups=ALONG_X)


def to_next_x(part, step):
    moves = [
        (z * NX + x, z * NX + (x + step) % NX) for z in range(NZ) for x in range(NX)
    ]
    return lax.ppermute(part, "pool", moves)


def over_con(parts):
    return lax.all_to_all(parts, "con", 0, 0, tiled=True)


def over_rows(parts):
    return lax.all_to_all(
        parts, ("pool", "con"), 0, 0, tiled=True, axis_index_groups=SAME_Z
    )


def call(body, outs, args, scratch=(), hbm=(), flops=0, trans=0):
    vmem = pl.BlockSpec(memory_space=pltpu.VMEM)
    nbytes = sum(a.size * a.dtype.itemsize for a in args) + sum(
        o.size * o.dtype.itemsize for o in outs
    )
    return pl.pallas_call(
        body,
        out_shape=outs,
        in_specs=[
            pl.BlockSpec(memory_space=pltpu.HBM) if i in hbm else vmem
            for i in range(len(args))
        ],
        out_specs=[vmem] * len(outs),
        scratch_shapes=list(scratch),
        compiler_params=pltpu.CompilerParams(vmem_limit_bytes=16 * 1024 * 1024),
        cost_estimate=pl.CostEstimate(
            flops=flops, bytes_accessed=nbytes, transcendentals=trans
        ),
    )(
        *(
            pltpu.with_memory_space_constraint(a, pltpu.HBM) if i in hbm else a
            for i, a in enumerate(args)
        )
    )


def shape(*dims, dtype=F32):
    return jax.ShapeDtypeStruct(dims, dtype)


def pack_body(*refs):
    out, sems = refs[4], refs[9]
    copies = [
        pltpu.make_async_copy(refs[i], refs[5 + i], sems.at[i]) for i in range(4)
    ]
    for copy in copies:
        copy.start()
    for copy in copies:
        copy.wait()
    feat_t, supply, grad, eligible = refs[5:9]
    rows = feat_t[...].astype(F32)
    for x in range(NX):
        out[x, :F, :] = rows
        out[x, F : F + 1, :] = supply[...]
        out[x, F + 1 : F + 2, :] = grad[...]
        for k in range(CG):
            for t in range(TILES_IN):
                out[x, MASK_AT + k : MASK_AT + k + 1, t * LANES : (t + 1) * LANES] = (
                    jnp.full((1, LANES), eligible[t, x * CG + k].astype(F32), F32)
                )
        out[x, MASK_AT + CG :, :] = jnp.zeros((PACK - MASK_AT - CG, ROWS_IN), F32)


def put_columns(row, out, copies):
    for k in range(CG):
        piece = row[:, k * LANES : (k + 1) * LANES]
        for w in range(copies):
            out[w, k : k + 1, :] = piece


def kernel_body(packed, cft, kern, kern16, supply, grad, sums, ones, acc):
    width = 256
    acc[...] = jnp.zeros_like(acc)
    for x in range(NX):
        for t in range(TILES_IN):
            at = slice(t * LANES, (t + 1) * LANES)
            g = x * TILES_IN + t
            supply[g : g + 1, :] = packed[x, F : F + 1, at]
            grad[g : g + 1, :] = packed[x, F + 1 : F + 2, at]

    def per_shard(x, _):
        for h in range(2):
            feat = packed[x, :F, h * 256 : h * 256 + 256].T.astype(BF16)
            base = pl.multiple_of(x * ROWS_IN + h * 256, 256)
            for n in range(COLS // width):
                scores = jnp.dot(
                    feat,
                    cft[:, n * width : (n + 1) * width],
                    preferred_element_type=F32,
                )
                values = jnp.exp2(scores * EXPONENT)
                for t in range(2):
                    for j in range(2):
                        k = n * 2 + j
                        tile = h * 2 + t
                        block = (
                            values[t * 128 : t * 128 + 128, j * 128 : j * 128 + 128]
                            * packed[
                                x,
                                MASK_AT + k : MASK_AT + k + 1,
                                tile * 128 : tile * 128 + 128,
                            ]
                        )
                        rows = pl.ds(base + t * 128, 128)
                        kern[rows, k * 128 : k * 128 + 128] = block
                        kern16[rows, k * 128 : k * 128 + 128] = block.astype(BF16)
                        acc[:, k * 128 : k * 128 + 128] += jnp.sum(
                            block.reshape(16, 8, 128), axis=0
                        )
        return 0

    lax.fori_loop(0, NX, per_shard, 0, unroll=4)
    put_columns(jnp.sum(acc[...], axis=0, keepdims=True), sums, NZ)
    feat = jnp.concatenate([packed[x, :F, :] for x in range(NX)], axis=1).astype(BF16)
    put_features(jnp.dot(feat, kern16[...], preferred_element_type=F32), ones)


def row_sums(kern, vec, out, copies):
    def group(g, _):
        rows = pl.ds(pl.multiple_of(g * LANES, LANES), LANES)
        total = kern[rows, 0:LANES] * vec[0:1, :]
        for k in range(1, CG):
            total += kern[rows, k * LANES : (k + 1) * LANES] * vec[k : k + 1, :]
        line = jnp.sum(total.T, axis=0, keepdims=True)
        for w in range(copies):
            out[w, pl.ds(g, 1), :] = line
        return 0

    lax.fori_loop(0, RG, group, 0, unroll=True)


def as_column(vec, g):
    return jnp.broadcast_to(vec[pl.ds(g, 1), :], (LANES, LANES)).T


def column_sums(kern, vec, out, copies):
    totals = [jnp.zeros((8, LANES), F32)] * CG
    for g in range(RG):
        rows = slice(g * LANES, (g + 1) * LANES)
        weight = as_column(vec, g)
        for k in range(CG):
            block = kern[rows, k * LANES : (k + 1) * LANES] * weight
            totals[k] += jnp.sum(block.reshape(16, 8, LANES), axis=0)
    line = jnp.concatenate(
        [jnp.sum(total, axis=0, keepdims=True) for total in totals], axis=1
    )
    put_columns(line, out, copies)


def forward_columns_body(gathered, demand, kern, scale, out):
    scale[...] = demand[...] / jnp.sum(gathered[...], axis=0)
    row_sums(kern, scale, out, NXC)


def second_columns_body(gathered, demand, kern, scale, ones, out):
    ones[...] = jnp.sum(gathered[:, :, :WIDE], axis=0)
    forward_columns_body(gathered.at[:, :, WIDE:], demand, kern, scale, out)


def adjoint_columns_body(gathered, demand, scale, grad, kern, adj, out):
    s = scale[...]
    summed = jnp.sum(gathered[...], axis=0)
    adj[...] = -(grad[...] / s + summed) * s * s / demand[...]
    row_sums(kern, adj, out, NXC)


def split(value):
    high = value.astype(BF16)
    return high, (value - high.astype(F32)).astype(BF16)


def feature_sums(packed, vecs, kern16):
    halves = []
    for vec in vecs:
        lines = [
            packed[g // TILES_IN, :F, g % TILES_IN * LANES : (g % TILES_IN + 1) * LANES]
            * vec[g : g + 1, :]
            for g in range(RG)
        ]
        halves += split(jnp.concatenate(lines, axis=1))
    sums = jnp.dot(
        jnp.concatenate(halves, axis=0), kern16[...], preferred_element_type=F32
    )
    return [
        sums[i * 2 * F : (i * 2 + 1) * F] + sums[(i * 2 + 1) * F : (i * 2 + 2) * F]
        for i in range(len(vecs))
    ]


def put_features(value, out):
    for z in range(NZ):
        f, half = z // 2 * 8, z % 2 * WIDE
        out[z] = value[f : f + 8, half : half + WIDE]


def forward_rows_body(
    gathered, supply, kern, ones, total, scale, out
):
    total[...] = jnp.sum(gathered[...], axis=0)
    scale[...] = supply[...] / total[...]
    out[:, :, :WIDE] = ones[...]
    column_sums(kern, scale, out.at[:, :, WIDE:], NZ)


def last_rows_body(gathered, grad, kern, adj, out):
    adj[...] = -grad[...] / jnp.sum(gathered[...], axis=0)
    column_sums(kern, adj, out, NZ)


def as_row(vec):
    return jnp.concatenate([vec[k : k + 1, :] for k in range(CG)], axis=1)


def inner_rows_body(
    gathered, scale, total, kern, kern16, packed, v1, v2, c2, adj2, adj, out
):
    adj[...] = -jnp.sum(gathered[...], axis=0) * scale[...] / total[...]
    with_adj2, with_scale, with_adj = feature_sums(packed, [adj2, scale, adj], kern16)
    put_features(
        as_row(v2) * with_adj2 + as_row(c2) * with_scale + as_row(v1) * with_adj,
        out.at[:, :, :WIDE],
    )
    column_sums(kern, adj, out.at[:, :, WIDE:], NZ)


def owner_body(gathered, ones, v1, demand, c1, out):
    v = v1[...]
    c1[...] = -jnp.sum(gathered[:, :, WIDE:], axis=0) * v * v / demand[...]
    scale = as_row(c1)
    odd = lax.rem(lax.div(lax.axis_index("pool"), NX), 2) == 1
    mine = jnp.where(odd, scale[:, WIDE:], scale[:, :WIDE]) * ones[...]
    value = (jnp.sum(gathered[:, :, :WIDE], axis=0) + mine) * 0.125
    for w in range(NZ):
        out[w] = value


def pool_part_body(c1, v1, v2, c2, adj2, u1, adj1, kern, cft, out, prod):
    def shard(x, _):
        for t in range(TILES_IN):
            g = x * TILES_IN + t
            rows = pl.ds(pl.multiple_of(g * LANES, LANES), LANES)
            a2, uu, a1 = as_column(adj2, g), as_column(u1, g), as_column(adj1, g)
            for k in range(CG):
                at = slice(k * LANES, (k + 1) * LANES)
                one = slice(k, k + 1)
                w = a2 * v2[one, :] + uu * c2[one, :] + a1 * v1[one, :] + c1[one, :]
                prod[t * LANES : (t + 1) * LANES, at] = (kern[rows, at] * w).astype(BF16)
        part = lax.dot_general(
            cft[...], prod[...], (((1,), (1,)), ((), ())), preferred_element_type=F32
        )
        for c in range(NCON):
            out[x * NCON + c] = part[c * 8 : c * 8 + 8, :] * 0.125
        return 0

    lax.fori_loop(0, NX, shard, 0)


def sum_copies_body(gathered, out):
    value = jnp.sum(gathered[...], axis=0)
    for w in range(out.shape[0]):
        out[w] = value


def contract_out_body(own, before, after, far, out):
    x = lax.rem(lax.axis_index("pool"), NX)

    for part, shift in ((own, 0), (before, NX - 1), (after, 1), (far, NX // 2)):
        base = lax.rem(x + shift, NX) * COLS
        for z in range(NZ):
            at = pl.ds(pl.multiple_of(base + z % 2 * WIDE, WIDE), WIDE)
            out[z // 2 * 8 : z // 2 * 8 + 8, at] = part[z]


def shards(pool_feat, contract_feat, supply, caps, eligible, grad_log_pool, grad_log_contract):
    x = lax.rem(lax.axis_index("pool"), NX)
    (packed,) = call(
        pack_body,
        [shape(NX, PACK, ROWS_IN)],
        [
            pool_feat.T,
            supply.reshape(1, -1),
            grad_log_pool.reshape(1, -1),
            eligible,
        ],
        scratch=[
            pltpu.VMEM((F, ROWS_IN), BF16),
            pltpu.VMEM((1, ROWS_IN), F32),
            pltpu.VMEM((1, ROWS_IN), F32),
            pltpu.SMEM((TILES_IN, NX * CG), jnp.int32),
            pltpu.SemaphoreType.DMA((4,)),
        ],
        hbm=(0, 1, 2, 3),
    )
    packed = over_x(packed)
    cft = lax.dynamic_slice_in_dim(contract_feat.T, x * COLS, COLS, 1)
    demand = lax.dynamic_slice_in_dim(caps.reshape(-1, LANES), x * CG, CG, 0).astype(F32)
    grad_c = lax.dynamic_slice_in_dim(grad_log_contract.reshape(-1, LANES), x * CG, CG, 0)

    acc = pltpu.VMEM((8, COLS), F32)
    col_vec, row_vec = shape(CG, LANES), shape(RG, LANES)
    to_z_both = shape(NZ, CG, WIDE + LANES)
    to_z, to_rows = shape(NZ, CG, LANES), shape(NXC, RG, LANES)
    size = ROWS * COLS

    packed, cft, demand, grad_c = lax.optimization_barrier((packed, cft, demand, grad_c))
    kern, kern16, a, grad_p, part, ones = call(
        kernel_body,
        [
            shape(ROWS, COLS),
            shape(ROWS, COLS, dtype=BF16),
            row_vec,
            row_vec,
            to_z,
            shape(NZ, 8, WIDE),
        ],
        [packed, cft],
        scratch=[acc],
        flops=size * 512,
        trans=size,
    )
    got = over_z(part)
    v1, part = call(
        forward_columns_body, [col_vec, to_rows], [got, demand, kern], flops=2 * size
    )
    got = over_rows(part)
    r1, u1, part = call(
        forward_rows_body,
        [row_vec, row_vec, to_z_both],
        [got, a, kern, ones],
        flops=2 * size,
    )
    got = over_z(part)
    v2, ones, part = call(
        second_columns_body,
        [col_vec, shape(8, WIDE), to_rows],
        [got, demand, kern],
        flops=2 * size,
    )
    got = over_rows(part)
    adj2, part = call(
        last_rows_body, [row_vec, to_z], [got, grad_p, kern], flops=2 * size
    )
    got = over_z(part)
    c2, part = call(
        adjoint_columns_body,
        [col_vec, to_rows],
        [got, demand, v2, grad_c, kern],
        flops=2 * size,
    )
    got = over_rows(part)
    adj1, part = call(
        inner_rows_body,
        [row_vec, to_z_both],
        [got, u1, r1, kern, kern16, packed, v1, v2, c2, adj2],
        flops=size * 512,
    )
    got = over_z(part)
    c1, owned = call(
        owner_body, [col_vec, shape(NZ, 8, WIDE)], [got, ones, v1, demand]
    )
    contract_got = over_z(owned)
    (pool_part,) = call(
        pool_part_body,
        [shape(NXC, 8, ROWS_IN)],
        [c1, v1, v2, c2, adj2, u1, adj1, kern, cft],
        scratch=[pltpu.VMEM((ROWS_IN, COLS), BF16)],
        flops=size * 512,
    )
    contract_got, pool_part = lax.optimization_barrier((contract_got, pool_part))
    pool_got = over_rows(pool_part)
    before, after = to_next_x(contract_got, 1), to_next_x(contract_got, -1)
    far = to_next_x(before, 1)
    (pool_copies,) = call(
        sum_copies_body, [shape(NCON, 8, ROWS_IN)], [pool_got]
    )
    pool_got = over_con(pool_copies)
    (contract_grad,) = call(
        contract_out_body,
        [shape(F, NX * COLS)],
        [contract_got, before, after, far],
    )
    return pool_got.reshape(F, ROWS_IN).T, contract_grad.T


def solution(mesh):
    placed = (
        P("pool", None),
        P("con", None),
        P("pool"),
        P("con"),
        P("pool", "con"),
        P("pool"),
        P("con"),
    )
    return jax.shard_map(
        shards,
        mesh=mesh,
        in_specs=placed,
        out_specs=(P("pool", None), P("con", None)),
        check_vma=False,
    )
```

```python
import math

import jax
import jax.numpy as jnp
from jax import lax
from jax.experimental import pallas as pl
from jax.experimental.pallas import tpu as pltpu
from jax.sharding import PartitionSpec as P

NX = 4
NZ = 16
NCON = 8
NXC = NX * NCON
LANES = 128
F = 64
ROWS_IN = 512
ROWS = NX * ROWS_IN
COLS = 1024
RG = ROWS // LANES
CG = COLS // LANES
TILES_IN = ROWS_IN // LANES
MASK_AT = F + 2
PACK = 80
WIDE = 512
EXPONENT = 0.125 * math.log2(math.e)
F32 = jnp.float32
BF16 = jnp.bfloat16

ALONG_Z = [[z * NX + x for z in range(NZ)] for x in range(NX)]
ALONG_X = [[z * NX + x for x in range(NX)] for z in range(NZ)]
SAME_Z = [[z * NXC + k for k in range(NXC)] for z in range(NZ)]

SAME_Z_AND_CORE = [
    [z * NXC + k for k in range(core, NXC, 2)] for z in range(NZ) for core in range(2)
]


def over_z(parts):
    return lax.all_to_all(parts, "pool", 0, 0, tiled=True, axis_index_groups=ALONG_Z)


def over_x(parts):
    return lax.all_to_all(parts, "pool", 0, 0, tiled=True, axis_index_groups=ALONG_X)


def to_next_x(part, step):
    moves = [
        (z * NX + x, z * NX + (x + step) % NX) for z in range(NZ) for x in range(NX)
    ]
    return lax.ppermute(part, "pool", moves)


def over_con(parts):
    return lax.all_to_all(parts, "con", 0, 0, tiled=True)


def over_xy(parts):
    return lax.all_to_all(
        parts, ("pool", "con"), 0, 0, tiled=True, axis_index_groups=SAME_Z_AND_CORE
    )


def to_other_core(part):
    return lax.ppermute(part, "con", [(c, c ^ 1) for c in range(NCON)])


def over_rows(parts):
    return lax.all_to_all(
        parts, ("pool", "con"), 0, 0, tiled=True, axis_index_groups=SAME_Z
    )


def call(body, outs, args, scratch=(), hbm=(), flops=0, trans=0):
    vmem = pl.BlockSpec(memory_space=pltpu.VMEM)
    nbytes = sum(a.size * a.dtype.itemsize for a in args) + sum(
        o.size * o.dtype.itemsize for o in outs
    )
    return pl.pallas_call(
        body,
        out_shape=outs,
        in_specs=[
            pl.BlockSpec(memory_space=pltpu.HBM) if i in hbm else vmem
            for i in range(len(args))
        ],
        out_specs=[vmem] * len(outs),
        scratch_shapes=list(scratch),
        compiler_params=pltpu.CompilerParams(vmem_limit_bytes=16 * 1024 * 1024),
        cost_estimate=pl.CostEstimate(
            flops=flops, bytes_accessed=nbytes, transcendentals=trans
        ),
    )(
        *(
            pltpu.with_memory_space_constraint(a, pltpu.HBM) if i in hbm else a
            for i, a in enumerate(args)
        )
    )


def shape(*dims, dtype=F32):
    return jax.ShapeDtypeStruct(dims, dtype)


def pack_body(*refs):
    out, sems = refs[4], refs[9]
    copies = [
        pltpu.make_async_copy(refs[i], refs[5 + i], sems.at[i]) for i in range(4)
    ]
    for copy in copies:
        copy.start()
    for copy in copies:
        copy.wait()
    feat_t, supply, grad, eligible = refs[5:9]
    rows = feat_t[...].astype(F32)
    for x in range(NX):
        out[x, :F, :] = rows
        out[x, F : F + 1, :] = supply[...]
        out[x, F + 1 : F + 2, :] = grad[...]
        for k in range(CG):
            for t in range(TILES_IN):
                out[x, MASK_AT + k : MASK_AT + k + 1, t * LANES : (t + 1) * LANES] = (
                    jnp.full((1, LANES), eligible[t, x * CG + k].astype(F32), F32)
                )
        out[x, MASK_AT + CG :, :] = jnp.zeros((PACK - MASK_AT - CG, ROWS_IN), F32)


def put_columns(row, out, copies):
    for k in range(CG):
        piece = row[:, k * LANES : (k + 1) * LANES]
        for w in range(copies):
            out[w, k : k + 1, :] = piece


def kernel_body(packed, cft, kern, kern16, supply, grad, sums, ones, acc):
    width = 256
    acc[...] = jnp.zeros_like(acc)
    for x in range(NX):
        for t in range(TILES_IN):
            at = slice(t * LANES, (t + 1) * LANES)
            g = x * TILES_IN + t
            supply[g : g + 1, :] = packed[x, F : F + 1, at]
            grad[g : g + 1, :] = packed[x, F + 1 : F + 2, at]

    def per_shard(x, _):
        for h in range(2):
            feat = packed[x, :F, h * 256 : h * 256 + 256].T.astype(BF16)
            base = pl.multiple_of(x * ROWS_IN + h * 256, 256)
            for n in range(COLS // width):
                scores = jnp.dot(
                    feat,
                    cft[:, n * width : (n + 1) * width],
                    preferred_element_type=F32,
                )
                values = jnp.exp2(scores * EXPONENT)
                for t in range(2):
                    for j in range(2):
                        k = n * 2 + j
                        tile = h * 2 + t
                        block = (
                            values[t * 128 : t * 128 + 128, j * 128 : j * 128 + 128]
                            * packed[
                                x,
                                MASK_AT + k : MASK_AT + k + 1,
                                tile * 128 : tile * 128 + 128,
                            ]
                        )
                        rows = pl.ds(base + t * 128, 128)
                        kern[rows, k * 128 : k * 128 + 128] = block
                        kern16[rows, k * 128 : k * 128 + 128] = block.astype(BF16)
                        acc[:, k * 128 : k * 128 + 128] += jnp.sum(
                            block.reshape(16, 8, 128), axis=0
                        )
        return 0

    lax.fori_loop(0, NX, per_shard, 0, unroll=4)
    put_columns(jnp.sum(acc[...], axis=0, keepdims=True), sums, NZ)
    feat = jnp.concatenate([packed[x, :F, :] for x in range(NX)], axis=1).astype(BF16)
    put_features(jnp.dot(feat, kern16[...], preferred_element_type=F32), ones)


def row_sums(kern, vec, out, copies):
    def group(g, _):
        rows = pl.ds(pl.multiple_of(g * LANES, LANES), LANES)
        total = kern[rows, 0:LANES] * vec[0:1, :]
        for k in range(1, CG):
            total += kern[rows, k * LANES : (k + 1) * LANES] * vec[k : k + 1, :]
        line = jnp.sum(total.T, axis=0, keepdims=True)
        for w in range(copies):
            out[w, pl.ds(g, 1), :] = line
        return 0

    lax.fori_loop(0, RG, group, 0, unroll=True)


def as_column(vec, g):
    return jnp.broadcast_to(vec[pl.ds(g, 1), :], (LANES, LANES)).T


def column_sums(kern, vec, out, copies):
    totals = [jnp.zeros((8, LANES), F32)] * CG
    for g in range(RG):
        rows = slice(g * LANES, (g + 1) * LANES)
        weight = as_column(vec, g)
        for k in range(CG):
            block = kern[rows, k * LANES : (k + 1) * LANES] * weight
            totals[k] += jnp.sum(block.reshape(16, 8, LANES), axis=0)
    line = jnp.concatenate(
        [jnp.sum(total, axis=0, keepdims=True) for total in totals], axis=1
    )
    put_columns(line, out, copies)


def forward_columns_body(gathered, demand, kern, scale, out):
    scale[...] = demand[...] / jnp.sum(gathered[...], axis=0)
    row_sums(kern, scale, out, NXC)


def second_columns_body(gathered, demand, kern, scale, ones, out):
    ones[...] = jnp.sum(gathered[:, :, :WIDE], axis=0)
    forward_columns_body(gathered.at[:, :, WIDE:], demand, kern, scale, out)


def adjoint_columns_body(gathered, demand, scale, grad, kern, adj, out):
    s = scale[...]
    summed = jnp.sum(gathered[...], axis=0)
    adj[...] = -(grad[...] / s + summed) * s * s / demand[...]
    row_sums(kern, adj, out, NXC)


def split(value):
    high = value.astype(BF16)
    return high, (value - high.astype(F32)).astype(BF16)


def feature_sums(packed, vecs, kern16):
    halves = []
    for vec in vecs:
        lines = [
            packed[g // TILES_IN, :F, g % TILES_IN * LANES : (g % TILES_IN + 1) * LANES]
            * vec[g : g + 1, :]
            for g in range(RG)
        ]
        halves += split(jnp.concatenate(lines, axis=1))
    sums = jnp.dot(
        jnp.concatenate(halves, axis=0), kern16[...], preferred_element_type=F32
    )
    return [
        sums[i * 2 * F : (i * 2 + 1) * F] + sums[(i * 2 + 1) * F : (i * 2 + 2) * F]
        for i in range(len(vecs))
    ]


def put_features(value, out):
    for z in range(NZ):
        f, half = z // 2 * 8, z % 2 * WIDE
        out[z] = value[f : f + 8, half : half + WIDE]


def forward_rows_body(
    gathered, supply, kern, ones, total, scale, out
):
    total[...] = jnp.sum(gathered[...], axis=0)
    scale[...] = supply[...] / total[...]
    out[:, :, :WIDE] = ones[...]
    column_sums(kern, scale, out.at[:, :, WIDE:], NZ)


def last_rows_body(gathered, grad, kern, adj, out):
    adj[...] = -grad[...] / jnp.sum(gathered[...], axis=0)
    column_sums(kern, adj, out, NZ)


def as_row(vec):
    return jnp.concatenate([vec[k : k + 1, :] for k in range(CG)], axis=1)


def inner_rows_body(
    gathered, scale, total, kern, kern16, packed, v1, v2, c2, adj2, adj, out
):
    adj[...] = -jnp.sum(gathered[...], axis=0) * scale[...] / total[...]
    with_adj2, with_scale, with_adj = feature_sums(packed, [adj2, scale, adj], kern16)
    put_features(
        as_row(v2) * with_adj2 + as_row(c2) * with_scale + as_row(v1) * with_adj,
        out.at[:, :, :WIDE],
    )
    column_sums(kern, adj, out.at[:, :, WIDE:], NZ)


def owner_body(gathered, ones, v1, demand, c1, out):
    v = v1[...]
    c1[...] = -jnp.sum(gathered[:, :, WIDE:], axis=0) * v * v / demand[...]
    scale = as_row(c1)
    odd = lax.rem(lax.div(lax.axis_index("pool"), NX), 2) == 1
    mine = jnp.where(odd, scale[:, WIDE:], scale[:, :WIDE]) * ones[...]
    value = (jnp.sum(gathered[:, :, :WIDE], axis=0) + mine) * 0.125
    for w in range(NZ):
        out[w] = value


def pool_part_body(c1, v1, v2, c2, adj2, u1, adj1, kern, cft, keep, send, prod, parts):
    core = lax.rem(lax.axis_index("con"), 2)
    for x in range(NX):
        for t in range(TILES_IN):
            g = x * TILES_IN + t
            rows = slice(g * LANES, (g + 1) * LANES)
            a2, uu, a1 = as_column(adj2, g), as_column(u1, g), as_column(adj1, g)
            for k in range(CG):
                at = slice(k * LANES, (k + 1) * LANES)
                one = slice(k, k + 1)
                w = a2 * v2[one, :] + uu * c2[one, :] + a1 * v1[one, :] + c1[one, :]
                prod[t * LANES : (t + 1) * LANES, at] = (kern[rows, at] * w).astype(BF16)
        parts[x] = 0.125 * lax.dot_general(
            cft[...], prod[...], (((1,), (1,)), ((), ())), preferred_element_type=F32
        )
        for y in range(NCON // 2):
            for mine, out in ((core, keep), (1 - core, send)):
                at = pl.ds(pl.multiple_of((2 * y + mine) * 8, 8), 8)
                out[x * (NCON // 2) + y] = parts[x, at, :]


def add_body(a, b, out):
    out[...] = a[...] + b[...]


def sum_copies_body(gathered, out):
    value = jnp.sum(gathered[...], axis=0)
    for w in range(out.shape[0]):
        out[w] = value


def contract_out_body(own, before, after, far, out):
    x = lax.rem(lax.axis_index("pool"), NX)

    for part, shift in ((own, 0), (before, NX - 1), (after, 1), (far, NX // 2)):
        base = lax.rem(x + shift, NX) * COLS
        for z in range(NZ):
            at = pl.ds(pl.multiple_of(base + z % 2 * WIDE, WIDE), WIDE)
            out[z // 2 * 8 : z // 2 * 8 + 8, at] = part[z]


def shards(pool_feat, contract_feat, supply, caps, eligible, grad_log_pool, grad_log_contract):
    x = lax.rem(lax.axis_index("pool"), NX)
    (packed,) = call(
        pack_body,
        [shape(NX, PACK, ROWS_IN)],
        [
            pool_feat.T,
            supply.reshape(1, -1),
            grad_log_pool.reshape(1, -1),
            eligible,
        ],
        scratch=[
            pltpu.VMEM((F, ROWS_IN), BF16),
            pltpu.VMEM((1, ROWS_IN), F32),
            pltpu.VMEM((1, ROWS_IN), F32),
            pltpu.SMEM((TILES_IN, NX * CG), jnp.int32),
            pltpu.SemaphoreType.DMA((4,)),
        ],
        hbm=(0, 1, 2, 3),
    )
    packed = over_x(packed)
    cft = lax.dynamic_slice_in_dim(contract_feat.T, x * COLS, COLS, 1)
    demand = lax.dynamic_slice_in_dim(caps.reshape(-1, LANES), x * CG, CG, 0).astype(F32)
    grad_c = lax.dynamic_slice_in_dim(grad_log_contract.reshape(-1, LANES), x * CG, CG, 0)

    acc = pltpu.VMEM((8, COLS), F32)
    col_vec, row_vec = shape(CG, LANES), shape(RG, LANES)
    to_z_both = shape(NZ, CG, WIDE + LANES)
    to_z, to_rows = shape(NZ, CG, LANES), shape(NXC, RG, LANES)
    size = ROWS * COLS

    packed, cft, demand, grad_c = lax.optimization_barrier((packed, cft, demand, grad_c))
    kern, kern16, a, grad_p, part, ones = call(
        kernel_body,
        [
            shape(ROWS, COLS),
            shape(ROWS, COLS, dtype=BF16),
            row_vec,
            row_vec,
            to_z,
            shape(NZ, 8, WIDE),
        ],
        [packed, cft],
        scratch=[acc],
        flops=size * 512,
        trans=size,
    )
    got = over_z(part)
    v1, part = call(
        forward_columns_body, [col_vec, to_rows], [got, demand, kern], flops=2 * size
    )
    got = over_rows(part)
    r1, u1, part = call(
        forward_rows_body,
        [row_vec, row_vec, to_z_both],
        [got, a, kern, ones],
        flops=2 * size,
    )
    got = over_z(part)
    v2, ones, part = call(
        second_columns_body,
        [col_vec, shape(8, WIDE), to_rows],
        [got, demand, kern],
        flops=2 * size,
    )
    got = over_rows(part)
    adj2, part = call(
        last_rows_body, [row_vec, to_z], [got, grad_p, kern], flops=2 * size
    )
    got = over_z(part)
    c2, part = call(
        adjoint_columns_body,
        [col_vec, to_rows],
        [got, demand, v2, grad_c, kern],
        flops=2 * size,
    )
    got = over_rows(part)
    adj1, part = call(
        inner_rows_body,
        [row_vec, to_z_both],
        [got, u1, r1, kern, kern16, packed, v1, v2, c2, adj2],
        flops=size * 512,
    )
    got = over_z(part)
    c1, owned = call(
        owner_body, [col_vec, shape(NZ, 8, WIDE)], [got, ones, v1, demand]
    )
    contract_got = over_z(owned)
    halves = shape(NXC // 2, 8, ROWS_IN)
    keep, send = call(
        pool_part_body,
        [halves, halves],
        [c1, v1, v2, c2, adj2, u1, adj1, kern, cft],
        scratch=[pltpu.VMEM((ROWS_IN, COLS), BF16), pltpu.VMEM((NX, F, ROWS_IN), F32)],
        flops=size * 512,
    )
    (pool_part,) = call(add_body, [halves], [keep, to_other_core(send)])
    contract_got, pool_part = lax.optimization_barrier((contract_got, pool_part))
    pool_got = over_xy(pool_part)
    before, after = to_next_x(contract_got, 1), to_next_x(contract_got, -1)
    far = to_next_x(before, 1)
    (pool_copies,) = call(
        sum_copies_body, [shape(NCON, 8, ROWS_IN)], [pool_got]
    )
    pool_got = over_con(pool_copies)
    (contract_grad,) = call(
        contract_out_body,
        [shape(F, NX * COLS)],
        [contract_got, before, after, far],
    )
    return pool_got.reshape(F, ROWS_IN).T, contract_grad.T


def solution(mesh):
    placed = (
        P("pool", None),
        P("con", None),
        P("pool"),
        P("con"),
        P("pool", "con"),
        P("pool"),
        P("con"),
    )
    return jax.shard_map(
        shards,
        mesh=mesh,
        in_specs=placed,
        out_specs=(P("pool", None), P("con", None)),
        check_vma=False,
    )
```

```python
import math

import jax
import jax.numpy as jnp
from jax import lax
from jax.experimental import pallas as pl
from jax.experimental.pallas import tpu as pltpu
from jax.sharding import PartitionSpec as P

NX = 4
NZ = 16
NCON = 8
NXC = NX * NCON
LANES = 128
F = 64
ROWS_IN = 512
ROWS = NX * ROWS_IN
COLS = 1024
RG = ROWS // LANES
CG = COLS // LANES
TILES_IN = ROWS_IN // LANES
MASK_AT = F + 2
PACK = 80
WIDE = 512
EXPONENT = 0.125 * math.log2(math.e)
F32 = jnp.float32
BF16 = jnp.bfloat16

ALONG_Z = [[z * NX + x for z in range(NZ)] for x in range(NX)]
ALONG_X = [[z * NX + x for x in range(NX)] for z in range(NZ)]
SAME_Z = [[z * NXC + k for k in range(NXC)] for z in range(NZ)]

SAME_Z_AND_CORE = [
    [z * NXC + k for k in range(core, NXC, 2)] for z in range(NZ) for core in range(2)
]


def over_z(parts):
    return lax.all_to_all(parts, "pool", 0, 0, tiled=True, axis_index_groups=ALONG_Z)


def over_x(parts):
    return lax.all_to_all(parts, "pool", 0, 0, tiled=True, axis_index_groups=ALONG_X)


def to_next_x(part, step):
    moves = [
        (z * NX + x, z * NX + (x + step) % NX) for z in range(NZ) for x in range(NX)
    ]
    return lax.ppermute(part, "pool", moves)


def over_con(parts):
    return lax.all_to_all(parts, "con", 0, 0, tiled=True)


def over_xy(parts):
    return lax.all_to_all(
        parts, ("pool", "con"), 0, 0, tiled=True, axis_index_groups=SAME_Z_AND_CORE
    )


def to_other_core(part):
    return lax.ppermute(part, "con", [(c, c ^ 1) for c in range(NCON)])


def over_rows(parts):
    return lax.all_to_all(
        parts, ("pool", "con"), 0, 0, tiled=True, axis_index_groups=SAME_Z
    )


def call(body, outs, args, scratch=(), hbm=(), flops=0, trans=0):
    vmem = pl.BlockSpec(memory_space=pltpu.VMEM)
    nbytes = sum(a.size * a.dtype.itemsize for a in args) + sum(
        o.size * o.dtype.itemsize for o in outs
    )
    return pl.pallas_call(
        body,
        out_shape=outs,
        in_specs=[
            pl.BlockSpec(memory_space=pltpu.HBM) if i in hbm else vmem
            for i in range(len(args))
        ],
        out_specs=[vmem] * len(outs),
        scratch_shapes=list(scratch),
        compiler_params=pltpu.CompilerParams(vmem_limit_bytes=16 * 1024 * 1024),
        cost_estimate=pl.CostEstimate(
            flops=flops, bytes_accessed=nbytes, transcendentals=trans
        ),
    )(
        *(
            pltpu.with_memory_space_constraint(a, pltpu.HBM) if i in hbm else a
            for i, a in enumerate(args)
        )
    )


def shape(*dims, dtype=F32):
    return jax.ShapeDtypeStruct(dims, dtype)


def pack_body(*refs):
    out, sems = refs[4], refs[9]
    copies = [
        pltpu.make_async_copy(refs[i], refs[5 + i], sems.at[i]) for i in range(4)
    ]
    for copy in copies:
        copy.start()
    for copy in copies:
        copy.wait()
    feat_t, supply, grad, eligible = refs[5:9]
    rows = feat_t[...].astype(F32)
    for x in range(NX):
        out[x, :F, :] = rows
        out[x, F : F + 1, :] = supply[...]
        out[x, F + 1 : F + 2, :] = grad[...]
        for k in range(CG):
            for t in range(TILES_IN):
                out[x, MASK_AT + k : MASK_AT + k + 1, t * LANES : (t + 1) * LANES] = (
                    jnp.full((1, LANES), eligible[t, x * CG + k].astype(F32), F32)
                )
        out[x, MASK_AT + CG :, :] = jnp.zeros((PACK - MASK_AT - CG, ROWS_IN), F32)


def put_columns(row, out, copies):
    for k in range(CG):
        piece = row[:, k * LANES : (k + 1) * LANES]
        for w in range(copies):
            out[w, k : k + 1, :] = piece


def kernel_body(packed, cft, kern, kern16, supply, grad, sums, ones, acc):
    width = 256
    acc[...] = jnp.zeros_like(acc)
    for x in range(NX):
        for t in range(TILES_IN):
            at = slice(t * LANES, (t + 1) * LANES)
            g = x * TILES_IN + t
            supply[g : g + 1, :] = packed[x, F : F + 1, at]
            grad[g : g + 1, :] = packed[x, F + 1 : F + 2, at]

    def per_shard(x, _):
        for h in range(2):
            feat = packed[x, :F, h * 256 : h * 256 + 256].T.astype(BF16)
            base = pl.multiple_of(x * ROWS_IN + h * 256, 256)
            for n in range(COLS // width):
                scores = jnp.dot(
                    feat,
                    cft[:, n * width : (n + 1) * width],
                    preferred_element_type=F32,
                )
                values = jnp.exp2(scores * EXPONENT)
                for t in range(2):
                    for j in range(2):
                        k = n * 2 + j
                        tile = h * 2 + t
                        block = (
                            values[t * 128 : t * 128 + 128, j * 128 : j * 128 + 128]
                            * packed[
                                x,
                                MASK_AT + k : MASK_AT + k + 1,
                                tile * 128 : tile * 128 + 128,
                            ]
                        )
                        rows = pl.ds(base + t * 128, 128)
                        kern[rows, k * 128 : k * 128 + 128] = block
                        kern16[rows, k * 128 : k * 128 + 128] = block.astype(BF16)
                        acc[:, k * 128 : k * 128 + 128] += jnp.sum(
                            block.reshape(16, 8, 128), axis=0
                        )
        return 0

    lax.fori_loop(0, NX, per_shard, 0, unroll=4)
    put_columns(
        jnp.sum(acc[...], axis=0, keepdims=True), sums.at[:, :, LANES:], NZ
    )
    feat = jnp.concatenate([packed[x, :F, :] for x in range(NX)], axis=1).astype(BF16)
    put_features(jnp.dot(feat, kern16[...], preferred_element_type=F32), ones)
    sums[:, :, :LANES] = ones[:, :, :LANES]


def row_sums(kern, vec, out, copies):
    def group(g, _):
        rows = pl.ds(pl.multiple_of(g * LANES, LANES), LANES)
        total = kern[rows, 0:LANES] * vec[0:1, :]
        for k in range(1, CG):
            total += kern[rows, k * LANES : (k + 1) * LANES] * vec[k : k + 1, :]
        line = jnp.sum(total.T, axis=0, keepdims=True)
        for w in range(copies):
            out[w, pl.ds(g, 1), :] = line
        return 0

    lax.fori_loop(0, RG, group, 0, unroll=True)


def as_column(vec, g):
    return jnp.broadcast_to(vec[pl.ds(g, 1), :], (LANES, LANES)).T


def column_sums(kern, vec, out, copies):
    totals = [jnp.zeros((8, LANES), F32)] * CG
    for g in range(RG):
        rows = slice(g * LANES, (g + 1) * LANES)
        weight = as_column(vec, g)
        for k in range(CG):
            block = kern[rows, k * LANES : (k + 1) * LANES] * weight
            totals[k] += jnp.sum(block.reshape(16, 8, LANES), axis=0)
    line = jnp.concatenate(
        [jnp.sum(total, axis=0, keepdims=True) for total in totals], axis=1
    )
    put_columns(line, out, copies)


def forward_columns_body(gathered, demand, kern, scale, ones, out):
    both = jnp.sum(gathered[...], axis=0)
    ones[...] = both[:, :-LANES]
    scale[...] = demand[...] / both[:, -LANES:]
    row_sums(kern, scale, out, NXC)


def adjoint_columns_body(gathered, demand, scale, grad, kern, adj, ones, out):
    s = scale[...]
    both = jnp.sum(gathered[...], axis=0)
    ones[...] = both[:, :-LANES]
    adj[...] = -(grad[...] / s + both[:, -LANES:]) * s * s / demand[...]
    row_sums(kern, adj, out, NXC)


def split(value):
    high = value.astype(BF16)
    return high, (value - high.astype(F32)).astype(BF16)


def feature_sums(packed, vecs, kern16):
    halves = []
    for vec in vecs:
        lines = [
            packed[g // TILES_IN, :F, g % TILES_IN * LANES : (g % TILES_IN + 1) * LANES]
            * vec[g : g + 1, :]
            for g in range(RG)
        ]
        halves += split(jnp.concatenate(lines, axis=1))
    sums = jnp.dot(
        jnp.concatenate(halves, axis=0), kern16[...], preferred_element_type=F32
    )
    return [
        sums[i * 2 * F : (i * 2 + 1) * F] + sums[(i * 2 + 1) * F : (i * 2 + 2) * F]
        for i in range(len(vecs))
    ]


def put_features(value, out):
    for z in range(NZ):
        f, half = z // 2 * 8, z % 2 * WIDE
        out[z] = value[f : f + 8, half : half + WIDE]


def forward_rows_body(
    gathered, supply, kern, ones, total, scale, out
):
    total[...] = jnp.sum(gathered[...], axis=0)
    scale[...] = supply[...] / total[...]
    out[:, :, : 2 * LANES] = ones[:, :, LANES : 3 * LANES]
    column_sums(kern, scale, out.at[:, :, 2 * LANES :], NZ)


def last_rows_body(gathered, grad, kern, ones, adj, out):
    adj[...] = -grad[...] / jnp.sum(gathered[...], axis=0)
    out[:, :, :LANES] = ones[:, :, 3 * LANES :]
    column_sums(kern, adj, out.at[:, :, LANES:], NZ)


def as_row(vec):
    return jnp.concatenate([vec[k : k + 1, :] for k in range(CG)], axis=1)


def inner_rows_body(
    gathered, scale, total, kern, kern16, packed, v1, v2, c2, adj2, adj, out
):
    adj[...] = -jnp.sum(gathered[...], axis=0) * scale[...] / total[...]
    with_adj2, with_scale, with_adj = feature_sums(packed, [adj2, scale, adj], kern16)
    put_features(
        as_row(v2) * with_adj2 + as_row(c2) * with_scale + as_row(v1) * with_adj,
        out.at[:, :, :WIDE],
    )
    column_sums(kern, adj, out.at[:, :, WIDE:], NZ)


def owner_body(gathered, first, second, third, v1, demand, c1, out):
    v = v1[...]
    c1[...] = -jnp.sum(gathered[:, :, WIDE:], axis=0) * v * v / demand[...]
    scale = as_row(c1)
    odd = lax.rem(lax.div(lax.axis_index("pool"), NX), 2) == 1
    ones = jnp.concatenate([first[...], second[...], third[...]], axis=1)
    mine = jnp.where(odd, scale[:, WIDE:], scale[:, :WIDE]) * ones
    value = (jnp.sum(gathered[:, :, :WIDE], axis=0) + mine) * 0.125
    for w in range(NZ):
        out[w] = value


def pool_part_body(c1, v1, v2, c2, adj2, u1, adj1, kern, cft, keep, send, prod, parts):
    core = lax.rem(lax.axis_index("con"), 2)
    for x in range(NX):
        for t in range(TILES_IN):
            g = x * TILES_IN + t
            rows = slice(g * LANES, (g + 1) * LANES)
            a2, uu, a1 = as_column(adj2, g), as_column(u1, g), as_column(adj1, g)
            for k in range(CG):
                at = slice(k * LANES, (k + 1) * LANES)
                one = slice(k, k + 1)
                w = a2 * v2[one, :] + uu * c2[one, :] + a1 * v1[one, :] + c1[one, :]
                prod[t * LANES : (t + 1) * LANES, at] = (kern[rows, at] * w).astype(BF16)
        parts[x] = 0.125 * lax.dot_general(
            cft[...], prod[...], (((1,), (1,)), ((), ())), preferred_element_type=F32
        )
        for y in range(NCON // 2):
            for mine, out in ((core, keep), (1 - core, send)):
                at = pl.ds(pl.multiple_of((2 * y + mine) * 8, 8), 8)
                out[x * (NCON // 2) + y] = parts[x, at, :]


def add_body(a, b, out):
    out[...] = a[...] + b[...]


def sum_copies_body(gathered, out):
    value = jnp.sum(gathered[...], axis=0)
    for w in range(out.shape[0]):
        out[w] = value


def contract_out_body(own, before, after, far, out):
    x = lax.rem(lax.axis_index("pool"), NX)

    for part, shift in ((own, 0), (before, NX - 1), (after, 1), (far, NX // 2)):
        base = lax.rem(x + shift, NX) * COLS
        for z in range(NZ):
            at = pl.ds(pl.multiple_of(base + z % 2 * WIDE, WIDE), WIDE)
            out[z // 2 * 8 : z // 2 * 8 + 8, at] = part[z]


def shards(pool_feat, contract_feat, supply, caps, eligible, grad_log_pool, grad_log_contract):
    x = lax.rem(lax.axis_index("pool"), NX)
    (packed,) = call(
        pack_body,
        [shape(NX, PACK, ROWS_IN)],
        [
            pool_feat.T,
            supply.reshape(1, -1),
            grad_log_pool.reshape(1, -1),
            eligible,
        ],
        scratch=[
            pltpu.VMEM((F, ROWS_IN), BF16),
            pltpu.VMEM((1, ROWS_IN), F32),
            pltpu.VMEM((1, ROWS_IN), F32),
            pltpu.SMEM((TILES_IN, NX * CG), jnp.int32),
            pltpu.SemaphoreType.DMA((4,)),
        ],
        hbm=(0, 1, 2, 3),
    )
    packed = over_x(packed)
    cft = lax.dynamic_slice_in_dim(contract_feat.T, x * COLS, COLS, 1)
    demand = lax.dynamic_slice_in_dim(caps.reshape(-1, LANES), x * CG, CG, 0).astype(F32)
    grad_c = lax.dynamic_slice_in_dim(grad_log_contract.reshape(-1, LANES), x * CG, CG, 0)

    acc = pltpu.VMEM((8, COLS), F32)
    col_vec, row_vec = shape(CG, LANES), shape(RG, LANES)
    to_z_both = shape(NZ, CG, WIDE + LANES)
    to_z_two, to_rows = shape(NZ, CG, 2 * LANES), shape(NXC, RG, LANES)
    size = ROWS * COLS

    packed, cft, demand, grad_c = lax.optimization_barrier((packed, cft, demand, grad_c))
    kern, kern16, a, grad_p, part, ones = call(
        kernel_body,
        [
            shape(ROWS, COLS),
            shape(ROWS, COLS, dtype=BF16),
            row_vec,
            row_vec,
            to_z_two,
            shape(NZ, 8, WIDE),
        ],
        [packed, cft],
        scratch=[acc],
        flops=size * 512,
        trans=size,
    )
    got = over_z(part)
    v1, first, part = call(
        forward_columns_body,
        [col_vec, shape(8, LANES), to_rows],
        [got, demand, kern],
        flops=2 * size,
    )
    got = over_rows(part)
    r1, u1, part = call(
        forward_rows_body,
        [row_vec, row_vec, shape(NZ, CG, 3 * LANES)],
        [got, a, kern, ones],
        flops=2 * size,
    )
    got = over_z(part)
    v2, second, part = call(
        forward_columns_body,
        [col_vec, shape(8, 2 * LANES), to_rows],
        [got, demand, kern],
        flops=2 * size,
    )
    got = over_rows(part)
    adj2, part = call(
        last_rows_body, [row_vec, to_z_two], [got, grad_p, kern, ones], flops=2 * size
    )
    got = over_z(part)
    c2, third, part = call(
        adjoint_columns_body,
        [col_vec, shape(8, LANES), to_rows],
        [got, demand, v2, grad_c, kern],
        flops=2 * size,
    )
    got = over_rows(part)
    adj1, part = call(
        inner_rows_body,
        [row_vec, to_z_both],
        [got, u1, r1, kern, kern16, packed, v1, v2, c2, adj2],
        flops=size * 512,
    )
    got = over_z(part)
    c1, owned = call(
        owner_body, [col_vec, shape(NZ, 8, WIDE)], [got, first, second, third, v1, demand]
    )
    contract_got = over_z(owned)
    halves = shape(NXC // 2, 8, ROWS_IN)
    keep, send = call(
        pool_part_body,
        [halves, halves],
        [c1, v1, v2, c2, adj2, u1, adj1, kern, cft],
        scratch=[pltpu.VMEM((ROWS_IN, COLS), BF16), pltpu.VMEM((NX, F, ROWS_IN), F32)],
        flops=size * 512,
    )
    (pool_part,) = call(add_body, [halves], [keep, to_other_core(send)])
    contract_got, pool_part = lax.optimization_barrier((contract_got, pool_part))
    pool_got = over_xy(pool_part)
    before, after = to_next_x(contract_got, 1), to_next_x(contract_got, -1)
    far = to_next_x(before, 1)
    (pool_copies,) = call(
        sum_copies_body, [shape(NCON, 8, ROWS_IN)], [pool_got]
    )
    pool_got = over_con(pool_copies)
    (contract_grad,) = call(
        contract_out_body,
        [shape(F, NX * COLS)],
        [contract_got, before, after, far],
    )
    return pool_got.reshape(F, ROWS_IN).T, contract_grad.T


def solution(mesh):
    placed = (
        P("pool", None),
        P("con", None),
        P("pool"),
        P("con"),
        P("pool", "con"),
        P("pool"),
        P("con"),
    )
    return jax.shard_map(
        shards,
        mesh=mesh,
        in_specs=placed,
        out_specs=(P("pool", None), P("con", None)),
        check_vma=False,
    )
```

```python
import math

import jax
import jax.numpy as jnp
from jax import lax
from jax.experimental import pallas as pl
from jax.experimental.pallas import tpu as pltpu
from jax.sharding import PartitionSpec as P

NX = 4
NZ = 16
NCON = 8
NXC = NX * NCON
LANES = 128
F = 64
ROWS_IN = 512
ROWS = NX * ROWS_IN
COLS = 1024
RG = ROWS // LANES
CG = COLS // LANES
TILES_IN = ROWS_IN // LANES
MASK_AT = F + 2
PACK = 80
WIDE = 512
EXPONENT = 0.125 * math.log2(math.e)
F32 = jnp.float32
BF16 = jnp.bfloat16

ALONG_Z = [[z * NX + x for z in range(NZ)] for x in range(NX)]
ALONG_X = [[z * NX + x for x in range(NX)] for z in range(NZ)]
SAME_Z = [[z * NXC + k for k in range(NXC)] for z in range(NZ)]

SAME_Z_AND_CORE = [
    [z * NXC + k for k in range(core, NXC, 2)] for z in range(NZ) for core in range(2)
]


def over_z(parts):
    return lax.all_to_all(parts, "pool", 0, 0, tiled=True, axis_index_groups=ALONG_Z)


def over_x(parts):
    return lax.all_to_all(parts, "pool", 0, 0, tiled=True, axis_index_groups=ALONG_X)


def to_next_x(part, step):
    moves = [
        (z * NX + x, z * NX + (x + step) % NX) for z in range(NZ) for x in range(NX)
    ]
    return lax.ppermute(part, "pool", moves)


def over_con(parts):
    return lax.all_to_all(parts, "con", 0, 0, tiled=True)


def over_xy(parts):
    return lax.all_to_all(
        parts, ("pool", "con"), 0, 0, tiled=True, axis_index_groups=SAME_Z_AND_CORE
    )


def to_other_core(part):
    return lax.ppermute(part, "con", [(c, c ^ 1) for c in range(NCON)])


def over_rows(parts):
    return lax.all_to_all(
        parts, ("pool", "con"), 0, 0, tiled=True, axis_index_groups=SAME_Z
    )


def call(body, outs, args, scratch=(), hbm=(), flops=0, trans=0):
    vmem = pl.BlockSpec(memory_space=pltpu.VMEM)
    nbytes = sum(a.size * a.dtype.itemsize for a in args) + sum(
        o.size * o.dtype.itemsize for o in outs
    )
    return pl.pallas_call(
        body,
        out_shape=outs,
        in_specs=[
            pl.BlockSpec(memory_space=pltpu.HBM) if i in hbm else vmem
            for i in range(len(args))
        ],
        out_specs=[vmem] * len(outs),
        scratch_shapes=list(scratch),
        compiler_params=pltpu.CompilerParams(vmem_limit_bytes=16 * 1024 * 1024),
        cost_estimate=pl.CostEstimate(
            flops=flops, bytes_accessed=nbytes, transcendentals=trans
        ),
    )(
        *(
            pltpu.with_memory_space_constraint(a, pltpu.HBM) if i in hbm else a
            for i, a in enumerate(args)
        )
    )


def shape(*dims, dtype=F32):
    return jax.ShapeDtypeStruct(dims, dtype)


def pack_body(*refs):
    out, sems = refs[4], refs[9]
    copies = [
        pltpu.make_async_copy(refs[i], refs[5 + i], sems.at[i]) for i in range(4)
    ]
    for copy in copies:
        copy.start()
    for copy in copies:
        copy.wait()
    feat_t, supply, grad, eligible = refs[5:9]
    rows = feat_t[...].astype(F32)
    for x in range(NX):
        out[x, :F, :] = rows
        out[x, F : F + 1, :] = supply[...]
        out[x, F + 1 : F + 2, :] = grad[...]
        for k in range(CG):
            for t in range(TILES_IN):
                out[x, MASK_AT + k : MASK_AT + k + 1, t * LANES : (t + 1) * LANES] = (
                    jnp.full((1, LANES), eligible[t, x * CG + k].astype(F32), F32)
                )
        out[x, MASK_AT + CG :, :] = jnp.zeros((PACK - MASK_AT - CG, ROWS_IN), F32)


def put_columns(row, out, copies):
    for k in range(CG):
        piece = row[:, k * LANES : (k + 1) * LANES]
        for w in range(copies):
            out[w, k : k + 1, :] = piece


def kernel_body(packed, cft, kern, kern16, supply, grad, sums, ones, acc):
    width = 256
    acc[...] = jnp.zeros_like(acc)
    for x in range(NX):
        for t in range(TILES_IN):
            at = slice(t * LANES, (t + 1) * LANES)
            g = x * TILES_IN + t
            supply[g : g + 1, :] = packed[x, F : F + 1, at]
            grad[g : g + 1, :] = packed[x, F + 1 : F + 2, at]

    def per_shard(x, _):
        for h in range(2):
            feat = packed[x, :F, h * 256 : h * 256 + 256].T.astype(BF16)
            base = pl.multiple_of(x * ROWS_IN + h * 256, 256)
            for n in range(COLS // width):
                scores = jnp.dot(
                    feat,
                    cft[:, n * width : (n + 1) * width],
                    preferred_element_type=F32,
                )
                values = jnp.exp2(scores * EXPONENT)
                for t in range(2):
                    for j in range(2):
                        k = n * 2 + j
                        tile = h * 2 + t
                        block = (
                            values[t * 128 : t * 128 + 128, j * 128 : j * 128 + 128]
                            * packed[
                                x,
                                MASK_AT + k : MASK_AT + k + 1,
                                tile * 128 : tile * 128 + 128,
                            ]
                        )
                        rows = pl.ds(base + t * 128, 128)
                        kern[rows, k * 128 : k * 128 + 128] = block
                        kern16[rows, k * 128 : k * 128 + 128] = block.astype(BF16)
                        acc[:, k * 128 : k * 128 + 128] += jnp.sum(
                            block.reshape(16, 8, 128), axis=0
                        )
        return 0

    lax.fori_loop(0, NX, per_shard, 0, unroll=4)
    put_columns(
        jnp.sum(acc[...], axis=0, keepdims=True), sums.at[:, :, LANES:], NZ
    )
    feat = jnp.concatenate([packed[x, :F, :] for x in range(NX)], axis=1).astype(BF16)
    put_features(jnp.dot(feat, kern16[...], preferred_element_type=F32), ones)
    sums[:, :, :LANES] = ones[:, :, :LANES]


def row_sums(kern, vec, out, copies):
    def group(g, _):
        rows = pl.ds(pl.multiple_of(g * LANES, LANES), LANES)
        total = kern[rows, 0:LANES] * vec[0:1, :]
        for k in range(1, CG):
            total += kern[rows, k * LANES : (k + 1) * LANES] * vec[k : k + 1, :]
        line = jnp.sum(total.T, axis=0, keepdims=True)
        for w in range(copies):
            out[w, pl.ds(g, 1), :] = line
        return 0

    lax.fori_loop(0, RG, group, 0, unroll=True)


def as_column(vec, g):
    return jnp.broadcast_to(vec[pl.ds(g, 1), :], (LANES, LANES)).T


def column_sums(kern, vec, out, copies):
    totals = [jnp.zeros((8, LANES), F32)] * CG
    for g in range(RG):
        rows = slice(g * LANES, (g + 1) * LANES)
        weight = as_column(vec, g)
        for k in range(CG):
            block = kern[rows, k * LANES : (k + 1) * LANES] * weight
            totals[k] += jnp.sum(block.reshape(16, 8, LANES), axis=0)
    line = jnp.concatenate(
        [jnp.sum(total, axis=0, keepdims=True) for total in totals], axis=1
    )
    put_columns(line, out, copies)


def forward_columns_body(gathered, demand, kern, scale, ones, out):
    both = jnp.sum(gathered[...], axis=0)
    ones[...] = both[:, :-LANES]
    scale[...] = demand[...] / both[:, -LANES:]
    row_sums(kern, scale, out, NXC)


def adjoint_columns_body(gathered, demand, scale, grad, kern, adj, ones, out):
    s = scale[...]
    both = jnp.sum(gathered[...], axis=0)
    ones[...] = both[:, :-LANES]
    adj[...] = -(grad[...] / s + both[:, -LANES:]) * s * s / demand[...]
    row_sums(kern, adj, out, NXC)


def split(value):
    high = value.astype(BF16)
    return high, (value - high.astype(F32)).astype(BF16)


def feature_sums(packed, vecs, kern16):
    halves = []
    for vec in vecs:
        lines = [
            packed[g // TILES_IN, :F, g % TILES_IN * LANES : (g % TILES_IN + 1) * LANES]
            * vec[g : g + 1, :]
            for g in range(RG)
        ]
        halves += split(jnp.concatenate(lines, axis=1))
    sums = jnp.dot(
        jnp.concatenate(halves, axis=0), kern16[...], preferred_element_type=F32
    )
    return [
        sums[i * 2 * F : (i * 2 + 1) * F] + sums[(i * 2 + 1) * F : (i * 2 + 2) * F]
        for i in range(len(vecs))
    ]


def put_features(value, out):
    for z in range(NZ):
        f, half = z // 2 * 8, z % 2 * WIDE
        out[z] = value[f : f + 8, half : half + WIDE]


def forward_rows_body(
    gathered, supply, kern, ones, total, scale, out
):
    total[...] = jnp.sum(gathered[...], axis=0)
    scale[...] = supply[...] / total[...]
    out[:, :, : 2 * LANES] = ones[:, :, LANES : 3 * LANES]
    column_sums(kern, scale, out.at[:, :, 2 * LANES :], NZ)


def last_rows_body(gathered, grad, kern, ones, adj, out):
    adj[...] = -grad[...] / jnp.sum(gathered[...], axis=0)
    out[:, :, :LANES] = ones[:, :, 3 * LANES :]
    column_sums(kern, adj, out.at[:, :, LANES:], NZ)


def as_row(vec):
    return jnp.concatenate([vec[k : k + 1, :] for k in range(CG)], axis=1)


def inner_rows_body(
    gathered, scale, total, kern, kern16, packed, v1, v2, c2, adj2, adj, out
):
    adj[...] = -jnp.sum(gathered[...], axis=0) * scale[...] / total[...]
    with_adj2, with_scale, with_adj = feature_sums(packed, [adj2, scale, adj], kern16)
    put_features(
        as_row(v2) * with_adj2 + as_row(c2) * with_scale + as_row(v1) * with_adj,
        out.at[:, :, :WIDE],
    )
    column_sums(kern, adj, out.at[:, :, WIDE:], NZ)


def owner_body(gathered, first, second, third, v1, demand, c1, out):
    v = v1[...]
    c1[...] = -jnp.sum(gathered[:, :, WIDE:], axis=0) * v * v / demand[...]
    scale = as_row(c1)
    odd = lax.rem(lax.div(lax.axis_index("pool"), NX), 2) == 1
    ones = jnp.concatenate([first[...], second[...], third[...]], axis=1)
    mine = jnp.where(odd, scale[:, WIDE:], scale[:, :WIDE]) * ones
    value = (jnp.sum(gathered[:, :, :WIDE], axis=0) + mine) * 0.125
    for w in range(NZ):
        out[w] = value


def pool_part_body(c1, v1, v2, c2, adj2, u1, adj1, kern, cft, keep, send, prod, parts):
    core = lax.rem(lax.axis_index("con"), 2)
    for x in range(NX):
        for t in range(TILES_IN):
            g = x * TILES_IN + t
            rows = slice(g * LANES, (g + 1) * LANES)
            a2, uu, a1 = as_column(adj2, g), as_column(u1, g), as_column(adj1, g)
            for k in range(CG):
                at = slice(k * LANES, (k + 1) * LANES)
                one = slice(k, k + 1)
                w = a2 * v2[one, :] + uu * c2[one, :] + a1 * v1[one, :] + c1[one, :]
                prod[t * LANES : (t + 1) * LANES, at] = (kern[rows, at] * w).astype(BF16)
        parts[x] = 0.125 * lax.dot_general(
            cft[...], prod[...], (((1,), (1,)), ((), ())), preferred_element_type=F32
        )
        for y in range(NCON // 2):
            for mine, out in ((core, keep), (1 - core, send)):
                at = pl.ds(pl.multiple_of((2 * y + mine) * 8, 8), 8)
                out[x * (NCON // 2) + y] = parts[x, at, :]


def add_body(a, b, out):
    out[...] = a[...] + b[...]


def sum_copies_body(gathered, out):
    value = jnp.sum(gathered[...], axis=0)
    for w in range(out.shape[0]):
        out[w] = value


def outputs_body(own, before, after, far, pool, out, pool_out):
    x = lax.rem(lax.axis_index("pool"), NX)

    for part, shift in ((own, 0), (before, NX - 1), (after, 1), (far, NX // 2)):
        base = lax.rem(x + shift, NX) * COLS
        for z in range(NZ):
            at = pl.ds(pl.multiple_of(base + z % 2 * WIDE, WIDE), WIDE)
            out[z // 2 * 8 : z // 2 * 8 + 8, at] = part[z]
    for c in range(NCON):
        pool_out[c * 8 : c * 8 + 8, :] = pool[c]


def shards(pool_feat, contract_feat, supply, caps, eligible, grad_log_pool, grad_log_contract):
    x = lax.rem(lax.axis_index("pool"), NX)
    (packed,) = call(
        pack_body,
        [shape(NX, PACK, ROWS_IN)],
        [
            pool_feat.T,
            supply.reshape(1, -1),
            grad_log_pool.reshape(1, -1),
            eligible,
        ],
        scratch=[
            pltpu.VMEM((F, ROWS_IN), BF16),
            pltpu.VMEM((1, ROWS_IN), F32),
            pltpu.VMEM((1, ROWS_IN), F32),
            pltpu.SMEM((TILES_IN, NX * CG), jnp.int32),
            pltpu.SemaphoreType.DMA((4,)),
        ],
        hbm=(0, 1, 2, 3),
    )
    packed = over_x(packed)
    cft = lax.dynamic_slice_in_dim(contract_feat.T, x * COLS, COLS, 1)
    demand = lax.dynamic_slice_in_dim(caps.reshape(-1, LANES), x * CG, CG, 0).astype(F32)
    grad_c = lax.dynamic_slice_in_dim(grad_log_contract.reshape(-1, LANES), x * CG, CG, 0)

    acc = pltpu.VMEM((8, COLS), F32)
    col_vec, row_vec = shape(CG, LANES), shape(RG, LANES)
    to_z_both = shape(NZ, CG, WIDE + LANES)
    to_z_two, to_rows = shape(NZ, CG, 2 * LANES), shape(NXC, RG, LANES)
    size = ROWS * COLS

    packed, cft, demand, grad_c = lax.optimization_barrier((packed, cft, demand, grad_c))
    kern, kern16, a, grad_p, part, ones = call(
        kernel_body,
        [
            shape(ROWS, COLS),
            shape(ROWS, COLS, dtype=BF16),
            row_vec,
            row_vec,
            to_z_two,
            shape(NZ, 8, WIDE),
        ],
        [packed, cft],
        scratch=[acc],
        flops=size * 512,
        trans=size,
    )
    got = over_z(part)
    v1, first, part = call(
        forward_columns_body,
        [col_vec, shape(8, LANES), to_rows],
        [got, demand, kern],
        flops=2 * size,
    )
    got = over_rows(part)
    r1, u1, part = call(
        forward_rows_body,
        [row_vec, row_vec, shape(NZ, CG, 3 * LANES)],
        [got, a, kern, ones],
        flops=2 * size,
    )
    got = over_z(part)
    v2, second, part = call(
        forward_columns_body,
        [col_vec, shape(8, 2 * LANES), to_rows],
        [got, demand, kern],
        flops=2 * size,
    )
    got = over_rows(part)
    adj2, part = call(
        last_rows_body, [row_vec, to_z_two], [got, grad_p, kern, ones], flops=2 * size
    )
    got = over_z(part)
    c2, third, part = call(
        adjoint_columns_body,
        [col_vec, shape(8, LANES), to_rows],
        [got, demand, v2, grad_c, kern],
        flops=2 * size,
    )
    got = over_rows(part)
    adj1, part = call(
        inner_rows_body,
        [row_vec, to_z_both],
        [got, u1, r1, kern, kern16, packed, v1, v2, c2, adj2],
        flops=size * 512,
    )
    got = over_z(part)
    c1, owned = call(
        owner_body, [col_vec, shape(NZ, 8, WIDE)], [got, first, second, third, v1, demand]
    )
    contract_got = over_z(owned)
    halves = shape(NXC // 2, 8, ROWS_IN)
    keep, send = call(
        pool_part_body,
        [halves, halves],
        [c1, v1, v2, c2, adj2, u1, adj1, kern, cft],
        scratch=[pltpu.VMEM((ROWS_IN, COLS), BF16), pltpu.VMEM((NX, F, ROWS_IN), F32)],
        flops=size * 512,
    )
    (pool_part,) = call(add_body, [halves], [keep, to_other_core(send)])
    contract_got, pool_part = lax.optimization_barrier((contract_got, pool_part))
    pool_got = over_xy(pool_part)
    before, after = to_next_x(contract_got, 1), to_next_x(contract_got, -1)
    far = to_next_x(before, 1)
    (pool_copies,) = call(
        sum_copies_body, [shape(NCON, 8, ROWS_IN)], [pool_got]
    )
    pool_got = over_con(pool_copies)
    contract_grad, pool_grad = call(
        outputs_body,
        [shape(F, NX * COLS), shape(F, ROWS_IN)],
        [contract_got, before, after, far, pool_got],
    )
    return pool_grad.T, contract_grad.T


def solution(mesh):
    placed = (
        P("pool", None),
        P("con", None),
        P("pool"),
        P("con"),
        P("pool", "con"),
        P("pool"),
        P("con"),
    )
    return jax.shard_map(
        shards,
        mesh=mesh,
        in_specs=placed,
        out_specs=(P("pool", None), P("con", None)),
        check_vma=False,
    )
```

```python
import math

import jax
import jax.numpy as jnp
from jax import lax
from jax.experimental import pallas as pl
from jax.experimental.pallas import tpu as pltpu
from jax.sharding import PartitionSpec as P

NX = 4
NZ = 16
NCON = 8
NXC = NX * NCON
LANES = 128
F = 64
ROWS_IN = 512
ROWS = NX * ROWS_IN
COLS = 1024
RG = ROWS // LANES
CG = COLS // LANES
TILES_IN = ROWS_IN // LANES
MASK_AT = F + 2
PACK = 72
WIDE = 512
EXPONENT = 0.125 * math.log2(math.e)
F32 = jnp.float32
BF16 = jnp.bfloat16

ALONG_Z = [[z * NX + x for z in range(NZ)] for x in range(NX)]
ALONG_X = [[z * NX + x for x in range(NX)] for z in range(NZ)]
SAME_Z = [[z * NXC + k for k in range(NXC)] for z in range(NZ)]

SAME_Z_AND_CORE = [
    [z * NXC + k for k in range(core, NXC, 2)] for z in range(NZ) for core in range(2)
]


def over_z(parts):
    return lax.all_to_all(parts, "pool", 0, 0, tiled=True, axis_index_groups=ALONG_Z)


def over_x(parts):
    return lax.all_to_all(parts, "pool", 0, 0, tiled=True, axis_index_groups=ALONG_X)


def to_next_x(part, step):
    moves = [
        (z * NX + x, z * NX + (x + step) % NX) for z in range(NZ) for x in range(NX)
    ]
    return lax.ppermute(part, "pool", moves)


def over_con(parts):
    return lax.all_to_all(parts, "con", 0, 0, tiled=True)


def over_xy(parts):
    return lax.all_to_all(
        parts, ("pool", "con"), 0, 0, tiled=True, axis_index_groups=SAME_Z_AND_CORE
    )


def to_other_core(part):
    return lax.ppermute(part, "con", [(c, c ^ 1) for c in range(NCON)])


def over_rows(parts):
    return lax.all_to_all(
        parts, ("pool", "con"), 0, 0, tiled=True, axis_index_groups=SAME_Z
    )


def call(body, outs, args, scratch=(), hbm=(), flops=0, trans=0):
    vmem = pl.BlockSpec(memory_space=pltpu.VMEM)
    nbytes = sum(a.size * a.dtype.itemsize for a in args) + sum(
        o.size * o.dtype.itemsize for o in outs
    )
    return pl.pallas_call(
        body,
        out_shape=outs,
        in_specs=[
            pl.BlockSpec(memory_space=pltpu.HBM) if i in hbm else vmem
            for i in range(len(args))
        ],
        out_specs=[vmem] * len(outs),
        scratch_shapes=list(scratch),
        compiler_params=pltpu.CompilerParams(vmem_limit_bytes=16 * 1024 * 1024),
        cost_estimate=pl.CostEstimate(
            flops=flops, bytes_accessed=nbytes, transcendentals=trans
        ),
    )(
        *(
            pltpu.with_memory_space_constraint(a, pltpu.HBM) if i in hbm else a
            for i, a in enumerate(args)
        )
    )


def shape(*dims, dtype=F32):
    return jax.ShapeDtypeStruct(dims, dtype)


def pack_body(*refs):
    out, sems = refs[4], refs[9]
    copies = [
        pltpu.make_async_copy(refs[i], refs[5 + i], sems.at[i]) for i in range(4)
    ]
    for copy in copies:
        copy.start()
    for copy in copies:
        copy.wait()
    feat_t, supply, grad, eligible = refs[5:9]
    rows = feat_t[...].astype(F32)
    lane = lax.broadcasted_iota(jnp.int32, (1, LANES), 1)
    for x in range(NX):
        out[x, :F, :] = rows
        out[x, F : F + 1, :] = supply[...]
        out[x, F + 1 : F + 2, :] = grad[...]
        mask = jnp.zeros((1, LANES), F32)
        for t in range(TILES_IN):
            for k in range(CG):
                mask = jnp.where(
                    lane == t * CG + k, eligible[t, x * CG + k].astype(F32), mask
                )
        out[x, MASK_AT:, :] = jnp.zeros((PACK - MASK_AT, ROWS_IN), F32)
        out[x, MASK_AT : MASK_AT + 1, :LANES] = mask


def put_columns(row, out, copies):
    for k in range(CG):
        piece = row[:, k * LANES : (k + 1) * LANES]
        for w in range(copies):
            out[w, k : k + 1, :] = piece


def kernel_body(packed, cft, kern, kern16, supply, grad, sums, ones, acc):
    width = 256
    acc[...] = jnp.zeros_like(acc)
    for x in range(NX):
        for t in range(TILES_IN):
            at = slice(t * LANES, (t + 1) * LANES)
            g = x * TILES_IN + t
            supply[g : g + 1, :] = packed[x, F : F + 1, at]
            grad[g : g + 1, :] = packed[x, F + 1 : F + 2, at]

    def per_shard(x, _):
        mask = packed[x, MASK_AT : MASK_AT + 1, :LANES]
        for h in range(2):
            feat = packed[x, :F, h * 256 : h * 256 + 256].T.astype(BF16)
            base = pl.multiple_of(x * ROWS_IN + h * 256, 256)
            for n in range(COLS // width):
                scores = jnp.dot(
                    feat,
                    cft[:, n * width : (n + 1) * width],
                    preferred_element_type=F32,
                )
                values = jnp.exp2(scores * EXPONENT)
                for t in range(2):
                    for j in range(2):
                        k = n * 2 + j
                        at = (h * 2 + t) * CG + k
                        block = (
                            values[t * 128 : t * 128 + 128, j * 128 : j * 128 + 128]
                            * jnp.broadcast_to(mask[:, at : at + 1], (1, LANES))
                        )
                        rows = pl.ds(base + t * 128, 128)
                        kern[rows, k * 128 : k * 128 + 128] = block
                        kern16[rows, k * 128 : k * 128 + 128] = block.astype(BF16)
                        acc[:, k * 128 : k * 128 + 128] += jnp.sum(
                            block.reshape(16, 8, 128), axis=0
                        )
        return 0

    lax.fori_loop(0, NX, per_shard, 0, unroll=4)
    put_columns(
        jnp.sum(acc[...], axis=0, keepdims=True), sums.at[:, :, LANES:], NZ
    )
    feat = jnp.concatenate([packed[x, :F, :] for x in range(NX)], axis=1).astype(BF16)
    put_features(jnp.dot(feat, kern16[...], preferred_element_type=F32), ones)
    sums[:, :, :LANES] = ones[:, :, :LANES]


def row_sums(kern, vec, out, copies):
    def group(g, _):
        rows = pl.ds(pl.multiple_of(g * LANES, LANES), LANES)
        total = kern[rows, 0:LANES] * vec[0:1, :]
        for k in range(1, CG):
            total += kern[rows, k * LANES : (k + 1) * LANES] * vec[k : k + 1, :]
        line = jnp.sum(total.T, axis=0, keepdims=True)
        for w in range(copies):
            out[w, pl.ds(g, 1), :] = line
        return 0

    lax.fori_loop(0, RG, group, 0, unroll=True)


def as_column(vec, g):
    return jnp.broadcast_to(vec[pl.ds(g, 1), :], (LANES, LANES)).T


def column_sums(kern, vec, out, copies):
    totals = [jnp.zeros((8, LANES), F32)] * CG
    for g in range(RG):
        rows = slice(g * LANES, (g + 1) * LANES)
        weight = as_column(vec, g)
        for k in range(CG):
            block = kern[rows, k * LANES : (k + 1) * LANES] * weight
            totals[k] += jnp.sum(block.reshape(16, 8, LANES), axis=0)
    line = jnp.concatenate(
        [jnp.sum(total, axis=0, keepdims=True) for total in totals], axis=1
    )
    put_columns(line, out, copies)


def forward_columns_body(gathered, demand, kern, scale, ones, out):
    both = jnp.sum(gathered[...], axis=0)
    ones[...] = both[:, :-LANES]
    scale[...] = demand[...] / both[:, -LANES:]
    row_sums(kern, scale, out, NXC)


def adjoint_columns_body(gathered, demand, scale, grad, kern, adj, ones, out):
    s = scale[...]
    both = jnp.sum(gathered[...], axis=0)
    ones[...] = both[:, :-LANES]
    adj[...] = -(grad[...] / s + both[:, -LANES:]) * s * s / demand[...]
    row_sums(kern, adj, out, NXC)


def split(value):
    high = value.astype(BF16)
    return high, (value - high.astype(F32)).astype(BF16)


def feature_sums(packed, vecs, kern16):
    halves = []
    for vec in vecs:
        lines = [
            packed[g // TILES_IN, :F, g % TILES_IN * LANES : (g % TILES_IN + 1) * LANES]
            * vec[g : g + 1, :]
            for g in range(RG)
        ]
        halves += split(jnp.concatenate(lines, axis=1))
    sums = jnp.dot(
        jnp.concatenate(halves, axis=0), kern16[...], preferred_element_type=F32
    )
    return [
        sums[i * 2 * F : (i * 2 + 1) * F] + sums[(i * 2 + 1) * F : (i * 2 + 2) * F]
        for i in range(len(vecs))
    ]


def put_features(value, out):
    for z in range(NZ):
        f, half = z // 2 * 8, z % 2 * WIDE
        out[z] = value[f : f + 8, half : half + WIDE]


def forward_rows_body(
    gathered, supply, kern, ones, total, scale, out
):
    total[...] = jnp.sum(gathered[...], axis=0)
    scale[...] = supply[...] / total[...]
    out[:, :, : 2 * LANES] = ones[:, :, LANES : 3 * LANES]
    column_sums(kern, scale, out.at[:, :, 2 * LANES :], NZ)


def last_rows_body(gathered, grad, kern, ones, adj, out):
    adj[...] = -grad[...] / jnp.sum(gathered[...], axis=0)
    out[:, :, :LANES] = ones[:, :, 3 * LANES :]
    column_sums(kern, adj, out.at[:, :, LANES:], NZ)


def as_row(vec):
    return jnp.concatenate([vec[k : k + 1, :] for k in range(CG)], axis=1)


def inner_rows_body(
    gathered, scale, total, kern, kern16, packed, v1, v2, c2, adj2, adj, out
):
    adj[...] = -jnp.sum(gathered[...], axis=0) * scale[...] / total[...]
    with_adj2, with_scale, with_adj = feature_sums(packed, [adj2, scale, adj], kern16)
    put_features(
        as_row(v2) * with_adj2 + as_row(c2) * with_scale + as_row(v1) * with_adj,
        out.at[:, :, :WIDE],
    )
    column_sums(kern, adj, out.at[:, :, WIDE:], NZ)


def owner_body(gathered, first, second, third, v1, demand, c1, out):
    v = v1[...]
    c1[...] = -jnp.sum(gathered[:, :, WIDE:], axis=0) * v * v / demand[...]
    scale = as_row(c1)
    odd = lax.rem(lax.div(lax.axis_index("pool"), NX), 2) == 1
    ones = jnp.concatenate([first[...], second[...], third[...]], axis=1)
    mine = jnp.where(odd, scale[:, WIDE:], scale[:, :WIDE]) * ones
    value = (jnp.sum(gathered[:, :, :WIDE], axis=0) + mine) * 0.125
    for w in range(NZ):
        out[w] = value


def pool_part_body(c1, v1, v2, c2, adj2, u1, adj1, kern, cft, keep, send, prod, parts):
    core = lax.rem(lax.axis_index("con"), 2)
    for x in range(NX):
        for t in range(TILES_IN):
            g = x * TILES_IN + t
            rows = slice(g * LANES, (g + 1) * LANES)
            a2, uu, a1 = as_column(adj2, g), as_column(u1, g), as_column(adj1, g)
            for k in range(CG):
                at = slice(k * LANES, (k + 1) * LANES)
                one = slice(k, k + 1)
                w = a2 * v2[one, :] + uu * c2[one, :] + a1 * v1[one, :] + c1[one, :]
                prod[t * LANES : (t + 1) * LANES, at] = (kern[rows, at] * w).astype(BF16)
        parts[x] = 0.125 * lax.dot_general(
            cft[...], prod[...], (((1,), (1,)), ((), ())), preferred_element_type=F32
        )
        for y in range(NCON // 2):
            for mine, out in ((core, keep), (1 - core, send)):
                at = pl.ds(pl.multiple_of((2 * y + mine) * 8, 8), 8)
                out[x * (NCON // 2) + y] = parts[x, at, :]


def add_body(a, b, out):
    out[...] = a[...] + b[...]


def sum_copies_body(gathered, out):
    value = jnp.sum(gathered[...], axis=0)
    for w in range(out.shape[0]):
        out[w] = value


def contract_out_body(own, before, after, far, out):
    x = lax.rem(lax.axis_index("pool"), NX)

    for part, shift in ((own, 0), (before, NX - 1), (after, 1), (far, NX // 2)):
        base = lax.rem(x + shift, NX) * COLS
        for z in range(NZ):
            at = pl.ds(pl.multiple_of(base + z % 2 * WIDE, WIDE), WIDE)
            out[z // 2 * 8 : z // 2 * 8 + 8, at] = part[z]


def shards(pool_feat, contract_feat, supply, caps, eligible, grad_log_pool, grad_log_contract):
    x = lax.rem(lax.axis_index("pool"), NX)
    (packed,) = call(
        pack_body,
        [shape(NX, PACK, ROWS_IN)],
        [
            pool_feat.T,
            supply.reshape(1, -1),
            grad_log_pool.reshape(1, -1),
            eligible,
        ],
        scratch=[
            pltpu.VMEM((F, ROWS_IN), BF16),
            pltpu.VMEM((1, ROWS_IN), F32),
            pltpu.VMEM((1, ROWS_IN), F32),
            pltpu.SMEM((TILES_IN, NX * CG), jnp.int32),
            pltpu.SemaphoreType.DMA((4,)),
        ],
        hbm=(0, 1, 2, 3),
    )
    packed = over_x(packed)
    cft = lax.dynamic_slice_in_dim(contract_feat.T, x * COLS, COLS, 1)
    demand = lax.dynamic_slice_in_dim(caps.reshape(-1, LANES), x * CG, CG, 0).astype(F32)
    grad_c = lax.dynamic_slice_in_dim(grad_log_contract.reshape(-1, LANES), x * CG, CG, 0)

    acc = pltpu.VMEM((8, COLS), F32)
    col_vec, row_vec = shape(CG, LANES), shape(RG, LANES)
    to_z_both = shape(NZ, CG, WIDE + LANES)
    to_z_two, to_rows = shape(NZ, CG, 2 * LANES), shape(NXC, RG, LANES)
    size = ROWS * COLS

    packed, cft, demand, grad_c = lax.optimization_barrier((packed, cft, demand, grad_c))
    kern, kern16, a, grad_p, part, ones = call(
        kernel_body,
        [
            shape(ROWS, COLS),
            shape(ROWS, COLS, dtype=BF16),
            row_vec,
            row_vec,
            to_z_two,
            shape(NZ, 8, WIDE),
        ],
        [packed, cft],
        scratch=[acc],
        flops=size * 512,
        trans=size,
    )
    got = over_z(part)
    v1, first, part = call(
        forward_columns_body,
        [col_vec, shape(8, LANES), to_rows],
        [got, demand, kern],
        flops=2 * size,
    )
    got = over_rows(part)
    r1, u1, part = call(
        forward_rows_body,
        [row_vec, row_vec, shape(NZ, CG, 3 * LANES)],
        [got, a, kern, ones],
        flops=2 * size,
    )
    got = over_z(part)
    v2, second, part = call(
        forward_columns_body,
        [col_vec, shape(8, 2 * LANES), to_rows],
        [got, demand, kern],
        flops=2 * size,
    )
    got = over_rows(part)
    adj2, part = call(
        last_rows_body, [row_vec, to_z_two], [got, grad_p, kern, ones], flops=2 * size
    )
    got = over_z(part)
    c2, third, part = call(
        adjoint_columns_body,
        [col_vec, shape(8, LANES), to_rows],
        [got, demand, v2, grad_c, kern],
        flops=2 * size,
    )
    got = over_rows(part)
    adj1, part = call(
        inner_rows_body,
        [row_vec, to_z_both],
        [got, u1, r1, kern, kern16, packed, v1, v2, c2, adj2],
        flops=size * 512,
    )
    got = over_z(part)
    c1, owned = call(
        owner_body, [col_vec, shape(NZ, 8, WIDE)], [got, first, second, third, v1, demand]
    )
    contract_got = over_z(owned)
    halves = shape(NXC // 2, 8, ROWS_IN)
    keep, send = call(
        pool_part_body,
        [halves, halves],
        [c1, v1, v2, c2, adj2, u1, adj1, kern, cft],
        scratch=[pltpu.VMEM((ROWS_IN, COLS), BF16), pltpu.VMEM((NX, F, ROWS_IN), F32)],
        flops=size * 512,
    )
    (pool_part,) = call(add_body, [halves], [keep, to_other_core(send)])
    contract_got, pool_part = lax.optimization_barrier((contract_got, pool_part))
    pool_got = over_xy(pool_part)
    before, after = to_next_x(contract_got, 1), to_next_x(contract_got, -1)
    far = to_next_x(before, 1)
    (pool_copies,) = call(
        sum_copies_body, [shape(NCON, 8, ROWS_IN)], [pool_got]
    )
    pool_got = over_con(pool_copies)
    (contract_grad,) = call(
        contract_out_body,
        [shape(F, NX * COLS)],
        [contract_got, before, after, far],
    )
    return pool_got.reshape(F, ROWS_IN).T, contract_grad.T


def solution(mesh):
    placed = (
        P("pool", None),
        P("con", None),
        P("pool"),
        P("con"),
        P("pool", "con"),
        P("pool"),
        P("con"),
    )
    return jax.shard_map(
        shards,
        mesh=mesh,
        in_specs=placed,
        out_specs=(P("pool", None), P("con", None)),
        check_vma=False,
    )
```
